512 devices in a mesh: wide: 64 (over y, z_hi, x), narrow: 8 (over z_lo, core).
Axes of the slice: x: 4, y: 4, z: 16 (z_hi: 4, z_lo: 4; z = z_hi * 4 + z_lo), core: 2. Of those that a mesh axis runs over, the one named last changes fastest.
Arguments:
- velocity: float32 [3, 128, 128, 128], P(None, 'wide', 'narrow'), may hold values from -6 to 6
- cotangents: float32 [4, 3, 128, 128, 128], P(None, None, 'wide', 'narrow'), may hold values from -6 to 6
- lead_table: float32 [8], replicated, may hold values from 0.25 to 4
- lead_index: int32 [4], replicated, may hold values from 0 to 7
- first_kernel: float32 [16, 3, 3, 3, 3], replicated, may hold values from -0.625 to 0.625
- first_bias: float32 [16], replicated, may hold values from -3 to 3
- second_kernel: float32 [3, 16, 3, 3, 3], replicated, may hold values from -0.3125 to 0.3125
Outputs:
- grad_velocity: float32 [3, 128, 128, 128], P(None, 'wide', 'narrow')
- grad_first_kernel: float32 [16, 3, 3, 3, 3], replicated
- grad_first_bias: float32 [16], replicated
- grad_second_kernel: float32 [3, 16, 3, 3, 3], replicated
The draws below stay inside these ranges and needn't reach their ends.
All inputs are finite; a program needn't handle non-finite values.
Results may differ from the reference program's by a relative error of at most 0.0003.
Values sent between devices are 32-bit elements; how exact they have to be, the bound alone decides.
A program may use at most 64 MiB of HBM per device.

```python
import math
import jax
import jax.numpy as jnp
from jax import lax

NX = 128
NY = 128
NZ = 128
CH = 16
LEADS = 4
HORIZONS = 8


def with_ends(values, stream_key, low, top_value):
    place = [jax.random.randint(jax.random.fold_in(stream_key, axis), (), 0, length) for axis, length in enumerate(values.shape)]
    longest = values.shape.index(max(values.shape))
    neighbour = place[:longest] + [(place[longest] + 1) % values.shape[longest]] + place[longest + 1:]
    return values.at[tuple(place)].set(low).at[tuple(neighbour)].set(top_value)


def shard_levels(rng, dims, pieces, low, high):
    def one(axis_at, shards_of):
        draws = jax.random.uniform(jax.random.fold_in(jax.random.fold_in(rng, 6), axis_at), (shards_of,), jnp.float32, low / len(pieces), high / len(pieces))
        return jnp.repeat(jnp.exp(draws), dims[axis_at] // shards_of).reshape((-1,) + (1,) * (len(dims) - axis_at - 1))

    factor_of = one(*pieces[0])
    for cut in pieces[1:]:
        factor_of = factor_of * one(*cut)
    return factor_of


def gaussian(own_key, dims, deviation, reach, shards=(), kind=jnp.bfloat16):
    array = jax.random.normal(own_key, dims, jnp.float32) * deviation
    if len(shards) > 0:
        array = shard_levels(own_key, dims, shards, -0.22, 0.18) * array
    return jnp.clip(array, min=-reach, max=reach).astype(kind)


def setup_inputs(seed: int = 0) -> dict:
    splits = jax.random.split(jax.random.key(seed), 8)
    velocity = gaussian(splits[0], (3, NX, NY, NZ), 1.0, 6.0, ((1, 64), (2, 8)), jnp.float32)
    cotangents = gaussian(splits[1], (LEADS, 3, NX, NY, NZ), 1.0, 6.0, ((2, 64), (3, 8)), jnp.float32)
    lead_table = jnp.clip(jnp.exp(jax.random.uniform(splits[2], (HORIZONS,), jnp.float32, math.log(0.25), math.log(4.0))), 0.25, 4.0)
    lead_index = with_ends(jax.random.randint(splits[3], (LEADS,), 0, HORIZONS), jax.random.fold_in(splits[3], 1), 0, HORIZONS - 1).astype(jnp.int32)
    first_kernel = gaussian(splits[4], (CH, 3, 3, 3, 3), 81 ** -0.5, 0.625, (), jnp.float32)
    first_bias = gaussian(splits[5], (CH,), 0.7, 3.0, (), jnp.float32)
    second_kernel = gaussian(splits[6], (3, CH, 3, 3, 3), (27 * CH) ** -0.5, 0.3125, (), jnp.float32)
    return {"velocity": velocity, "cotangents": cotangents, "lead_table": lead_table, "lead_index": lead_index, "first_kernel": first_kernel, "first_bias": first_bias, "second_kernel": second_kernel}


STEP_SIZE = 0.25

def advect(field):
    total = jnp.zeros_like(field)
    for j in range(3):
        before = jnp.roll(field, 1, j + 1)
        after = jnp.roll(field, -1, j + 1)
        total = total + jnp.maximum(field[j], 0.0) * (field - before) + jnp.minimum(field[j], 0.0) * (after - field)
    return field - STEP_SIZE * total

def correlate(field, kernel):
    padded = jnp.pad(field, ((0, 0), (1, 1), (1, 1), (1, 1)), mode='wrap')
    result = lax.conv_general_dilated(padded[None], kernel, (1, 1, 1), 'VALID', dimension_numbers=('NCDHW', 'OIDHW', 'NCDHW'), precision=lax.Precision.HIGHEST)
    return result[0]

def corrected(velocity, first_kernel, first_bias, second_kernel):
    advected = advect(velocity)
    hidden = jnp.tanh(correlate(advected, first_kernel) + first_bias[:, None, None, None])
    return advected + correlate(hidden, second_kernel)

def waves(length):
    index = jnp.arange(length, dtype=jnp.int32)
    return jnp.where(2 * index < length, index, index - length).astype(jnp.float32)

def project(field):
    spectrum = jnp.fft.fftn(field, axes=(1, 2, 3))
    wave_x = waves(NX)[:, None, None]
    wave_y = waves(NY)[None, :, None]
    wave_z = waves(NZ)[None, None, :]
    denom = jnp.maximum(wave_x * wave_x + wave_y * wave_y + wave_z * wave_z, 1.0)
    ratio = (wave_x * spectrum[0] + wave_y * spectrum[1] + wave_z * spectrum[2]) / denom
    spectrum = jnp.stack([spectrum[0] - wave_x * ratio, spectrum[1] - wave_y * ratio, spectrum[2] - wave_z * ratio])
    return jnp.real(jnp.fft.ifftn(spectrum, axes=(1, 2, 3)))

def reference(velocity, cotangents, lead_table, lead_index, first_kernel, first_bias, second_kernel):
    picks = lead_index[:, None] == jnp.arange(HORIZONS, dtype=jnp.int32)[None, :]
    weights = lax.optimization_barrier(jnp.sum(jnp.where(picks, lead_table[None, :], 0.0), axis=1))
    combined = jnp.einsum('l,lcxyz->cxyz', weights, cotangents, precision=lax.Precision.HIGHEST)
    projected = project(combined)
    outputs, pull = jax.vjp(corrected, velocity, first_kernel, first_bias, second_kernel)
    grad_velocity, grad_first, grad_bias, grad_second = pull(projected)
    factor = (NX * NY * NZ) ** (-0.5)
    return (grad_velocity, grad_first * factor, grad_bias * factor, grad_second * factor)
```

```python
import math

import jax
import jax.numpy as jnp
import ml_dtypes
import numpy as np
from jax import lax
from jax.experimental import pallas as pl
from jax.experimental.pallas import tpu as pltpu
from jax.sharding import PartitionSpec as P

F32 = jnp.float32
BF16 = jnp.bfloat16
MESH = pl.DeviceIdType.MESH
N = 128
WIDE = 64
NARROW = 8
STEP = 0.25


def basis(kind, wave):
    cell = np.arange(N)
    if kind == 0 and wave == 0:
        return np.full(N, 1.0 / math.sqrt(N))
    if kind == 1 and wave == 0:
        return (1.0 - 2.0 * (cell % 2)) / math.sqrt(N)
    angle = 2.0 * np.pi * (cell * wave % N) / N
    return math.sqrt(2.0 / N) * (np.cos(angle) if kind == 0 else np.sin(angle))


def halves(table):
    high = table.astype(np.float32).astype(ml_dtypes.bfloat16)
    low = (table - high.astype(np.float64)).astype(np.float32).astype(ml_dtypes.bfloat16)
    return np.stack([high, low])


def tables():
    tz = np.stack([basis(i % 2, i // 2) for i in range(N)])
    tx = np.stack([basis((i % 16) // 8, 8 * (i // 16) + i % 8) for i in range(N)])
    ty = np.stack([basis(i // 64, i % 64) for i in range(N)])
    ex = np.concatenate([tx[:, 0::2], tx[:, 1::2]], axis=0)
    rows = []
    for n in range(NARROW):
        cells = [16 * n + r for r in range(16)] + [16 * n - 1, 16 * n + 16]
        for y in cells:
            rows.append(ty[:, y % N])
        rows.extend([np.zeros(N)] * 6)
    tyi = np.stack(rows)
    txi = np.stack([tx[:, (2 * w - 1 + x) % N] for w in range(WIDE) for x in range(4)])
    zi = np.concatenate([tz[0::2], tz[1::2]], axis=1)
    spread = np.zeros((2, 2, N, 256))
    gather = np.zeros((2, 2, 144, N))
    for x in range(2):
        for c in range(3):
            for dx in range(3):
                for dy in range(3):
                    for dz in range(3):
                        flat = c * 27 + dx * 9 + dy * 3 + dz
                        lane = (dy * 3 + dz) * 16 + 4 * (x + dx) + c
                        back = ((2 - dy) * 3 + 2 - dz) * 16 + 4 * (x + 2 - dx) + c
                        spread[0, x, flat, lane] = 1.0
                        spread[1, x, flat, back] = 1.0
                        gather[0, x, lane, flat] = 1.0
                        gather[1, x, back, flat] = 1.0
        spread[0, x, 81, 4 * 16 + 3] = 1.0
        gather[0, x, 4 * 16 + 3, 81] = 1.0
    exact = ml_dtypes.bfloat16
    return (
        halves(tz),
        halves(ex),
        halves(ty),
        halves(tyi),
        halves(txi),
        halves(zi),
        spread.astype(exact),
        gather.astype(exact),
    )


def split(value):
    high = value.astype(BF16)
    return high, (value - high.astype(F32)).astype(BF16)


def dot(a, b, dims):
    return lax.dot_general(
        a, b, (((dims[0],), (dims[1],)), ((), ())), preferred_element_type=F32
    )


def dot3(a, b, dims=(1, 0)):
    return dot(a[0], b[0], dims) + dot(a[0], b[1], dims) + dot(a[1], b[0], dims)


def both(ref):
    return ref[0], ref[1]


def roll(value, shift):
    return pltpu.roll(value, shift % value.shape[1], 1)


def lanes():
    return lax.broadcasted_iota(jnp.int32, (1, N), 1)


def swap_blocks(m):
    m = m.T
    lane = lanes()
    for bit in (1, 2, 4):
        size = 16 * bit
        odd = (lane // size) % 2 == 1
        parts = []
        for i in range(0, N, 2 * size):
            low, high = m[i : i + size], m[i + size : i + 2 * size]
            parts.append(jnp.where(odd, roll(high, size), low))
            parts.append(jnp.where(odd, high, roll(low, -size)))
        m = jnp.concatenate(parts, axis=0)
    return m


def x_transform(received, ex):
    pair = jnp.concatenate(received, axis=1)
    big = dot3(ex, split(pair))
    lane = lanes()
    first = big[:N, :N] + roll(big[N:, :N], -48)
    second = roll(big[:N, N:], 48) + big[N:, N:]
    return jnp.where(lane < 48, first, jnp.where(lane < 96, second, 0.0))


def project(field, w, n):
    lane = lanes()
    row = lax.broadcasted_iota(jnp.int32, (N, 1), 0)
    block = lane // 16
    comp = block % 3
    is_sin_z = block // 3 % 2 == 1
    slot = lane % 16
    inside = lane < 96
    wave_x = 8 * n + slot % 8
    nyq_x = jnp.logical_and(slot == 8, n == 0)
    nyq_y = row == 64
    nyq_z = jnp.logical_and(is_sin_z, w == 0)
    kx = jnp.where(nyq_x, 64, wave_x).astype(F32)
    ky = jnp.where(nyq_y, 64, row % 64).astype(F32)
    kz = jnp.where(nyq_z, 64, w).astype(F32)
    inverse = 1.0 / jnp.maximum(kx * kx + ky * ky + kz * kz, 1.0)
    dx = jnp.where(slot < 8, wave_x, -wave_x).astype(F32)
    dy = jnp.where(row < 64, row % 64, -(row % 64)).astype(F32)
    dz = jnp.where(is_sin_z, -w, w).astype(F32)
    nyquist = jnp.where(
        comp == 0,
        jnp.where(nyq_x, 64.0, 0.0),
        jnp.where(comp == 2, jnp.where(nyq_z, 64.0, 0.0), 0.0),
    )
    nyquist = nyquist + jnp.where(jnp.logical_and(comp == 1, nyq_y), 64.0, 0.0)

    def derive(v):
        along_x = dx * jnp.where(slot < 8, roll(v, -8), roll(v, 8))
        along_y = dy * jnp.concatenate([v[64:], v[:64]], axis=0)
        along_z = dz * jnp.where(is_sin_z, roll(v, 48), roll(v, -48))
        return jnp.where(comp == 0, along_x, jnp.where(comp == 1, along_y, along_z))

    def over_components(v):
        total = (v + roll(v, -16) + roll(v, -32)) * inverse
        total = jnp.where(jnp.logical_and(inside, comp == 0), total, 0.0)
        return total + roll(total, 16) + roll(total, 32)

    main = over_components(derive(field))
    rest = over_components(nyquist * field)
    return field + derive(main) - nyquist * rest


def pack_rows(received):
    lane = lanes()
    inner = jnp.concatenate([received[24 * i : 24 * i + 16] for i in range(NARROW)], axis=0)
    none = jnp.zeros((8, N), F32)
    outer = []
    for i in range(NARROW):
        outer.extend([received[24 * i + 16 : 24 * i + 24], none])
    inner = swap_blocks(inner)
    outer = swap_blocks(jnp.concatenate(outer, axis=0))
    full = jnp.where(lane < 96, inner, 0.0)
    for k in range(2):
        for c in range(3):
            place = 96 + 8 * k + 2 * c
            here = jnp.logical_and(lane >= place, lane < place + 2)
            full = jnp.where(here, roll(outer, place - 16 * (3 * k + c)), full)
    return full


def taps(field, high_ref, low_ref):
    for dz in range(3):
        moved = field if dz == 1 else roll(field, 1 - dz)
        for ref, part in zip((high_ref, low_ref), split(moved)):
            for dy in range(3):
                at = (3 * dy + dz) * 16
                for y in range(16):
                    ref[at : at + 16, N * y : N * y + N] = part[16 * (y + dy) : 16 * (y + dy) + 16]


def shift_rows(value, by):
    return pltpu.roll(value, by % value.shape[0], 0)


def kernel(
    cot, vel, table, index, kcat, tz, ex, ty, tyi, txi, zi, spread, gather,
    out, sums,
    send1, recv1, send2, recv2, send3, recv3, send4, recv4,
    part, recv5, mine, recv6, whole, recv7,
    vext, adv, proj, proj_own, adv_hi, adv_lo, proj_hi, proj_lo,
    hidden, scattered, gpart, gnat, face_x, face_y, corner, gext,
    own_sem, send_sem, recv_sem, vel_send, vel_recv, e1_send, e1_recv, e2_send, e2_recv,
):
    w = lax.axis_index("wide")
    n = lax.axis_index("narrow")
    wy, wz, wx = w // 16, w // 4 % 4, w % 4
    right, left = lax.rem(w + 1, WIDE), lax.rem(w + WIDE - 1, WIDE)
    above, below = lax.rem(n + 1, NARROW), lax.rem(n + NARROW - 1, NARROW)

    def each_wide(act):
        for oz in (2, 1, 3, 0):

            def body(i, carry, oz=oz):
                oy, ox = i // 4, i % 4
                act(lax.rem(wy + oy, 4) * 16 + lax.rem(wz + oz, 4) * 4 + lax.rem(wx + ox, 4))
                return carry

            lax.fori_loop(1 if oz == 0 else 0, 16, body, 0)

    def each_narrow(act):
        def body(i, carry):
            act(lax.rem(n + i, NARROW))
            return carry

        lax.fori_loop(1, NARROW, body, 0)

    barrier = pltpu.get_barrier_semaphore()

    def greet(device):
        pl.semaphore_signal(barrier, inc=1, device_id=device, device_id_type=MESH)

    each_wide(lambda p: greet((p, n)))
    each_narrow(lambda p: greet((w, p)))
    diagonal = ((right, above), (right, below), (left, above), (left, below))
    for device in diagonal:
        greet(device)

    weight = [table[index[l]] for l in range(4)]
    pieces = []
    for x in range(2):
        for c in range(3):
            total = weight[0] * cot[0, c, x]
            for l in range(1, 4):
                total = total + weight[l] * cot[l, c, x]
            pieces.append(total)
    pieces.append(jnp.zeros((32, N), F32))
    combined = jnp.concatenate(pieces, axis=0)
    send1[...] = dot3(both(tz), split(combined), (1, 1))

    pl.semaphore_wait(barrier, WIDE - 1 + NARROW - 1 + 4)

    def exchange(k, axis, rows, source, target):
        size, me = (WIDE, w) if axis == "wide" else (NARROW, n)

        def block(ref, p):
            return ref.at[pl.ds(p * rows, rows)]

        def act(p):
            device = (p, n) if axis == "wide" else (w, p)
            pltpu.make_async_remote_copy(
                source if source.shape[0] == rows else block(source, p),
                block(target, me),
                send_sem.at[k],
                recv_sem.at[k],
                device_id=device,
                device_id_type=MESH,
            ).start()

        (each_wide if axis == "wide" else each_narrow)(act)
        own = pltpu.make_async_copy(
            source if source.shape[0] == rows else block(source, me), block(target, me), own_sem.at[k]
        )
        own.start()
        some = target.at[pl.ds(0, (size - 1) * rows)]
        device = (right, n) if axis == "wide" else (w, above)
        rest = pltpu.make_async_remote_copy(
            some, some, send_sem.at[k], recv_sem.at[k], device_id=device, device_id_type=MESH
        )

        def arrived():
            own.wait()
            rest.wait_recv()

        return arrived, rest.wait_send

    got1, sent1 = exchange(0, "wide", 2, send1, recv1)

    def copies(moves, sends, recvs):
        made = []
        for i, (source, target, device) in enumerate(moves):
            made.append(
                pltpu.make_async_remote_copy(
                    source, target, sends.at[i], recvs.at[i], device_id=device, device_id_type=MESH
                )
            )
        for copy in made:
            copy.start()
        return made

    low, high, full = pl.ds(0, 8), pl.ds(8, 8), pl.ds(0, 16)
    moves = []
    for device, rows, xs, ys in (
        ((right, n), full, 0, pl.ds(8, 16)),
        ((left, n), full, 4, pl.ds(8, 16)),
        ((w, above), high, 2, pl.ds(0, 8)),
        ((w, below), low, 2, pl.ds(24, 8)),
        ((right, above), high, 0, pl.ds(0, 8)),
        ((right, below), low, 0, pl.ds(24, 8)),
        ((left, above), high, 4, pl.ds(0, 8)),
        ((left, below), low, 4, pl.ds(24, 8)),
    ):
        moves.append((vel.at[:, :, rows, :], vext.at[:, pl.ds(xs, 2), ys, :], device))
    vel_copies = copies(moves, vel_send, vel_recv)
    vext[:, 2:4, 8:24, :] = vel[...]

    taps_first = []
    taps_second = []
    for part_of_kernel in split(kcat[...]):
        for place, kind in ((taps_first, 0), (taps_second, 1)):
            rows = part_of_kernel[16 * kind : 16 * kind + 16]
            place.append(
                jnp.concatenate(
                    [dot(rows, spread[kind, x], (1, 0))[:, :144] for x in range(2)], axis=0
                ).astype(BF16)
            )

    proj[...] = jnp.zeros_like(proj)
    gnat[...] = jnp.zeros_like(gnat)
    sublane = lax.broadcasted_iota(jnp.int32, (288, N), 0) % 16
    adv[...] = jnp.where(sublane == 3, 1.0, 0.0)

    for copy in vel_copies:
        copy.wait_recv()
    for x in range(4):
        v = [vext[c, x + 1] for c in range(3)]
        totals = [jnp.zeros((32, N), F32)] * 3
        for j in range(3):
            positive, negative = jnp.maximum(v[j], 0.0), jnp.minimum(v[j], 0.0)
            for c in range(3):
                if j == 0:
                    before, after = vext[c, x], vext[c, x + 2]
                elif j == 1:
                    before, after = shift_rows(v[c], 1), shift_rows(v[c], -1)
                else:
                    before, after = roll(v[c], 1), roll(v[c], -1)
                totals[c] = totals[c] + positive * (v[c] - before) + negative * (after - v[c])
        for c in range(3):
            done = v[c] - STEP * totals[c]
            at = 4 * x + c
            adv[at : at + 1] = done[7:8]
            adv[pl.ds(16 + at, 16, stride=16), :] = done[8:24]
            adv[272 + at : 273 + at] = done[24:25]
    taps(adv[...], adv_hi, adv_lo)
    adv_taps = (adv_hi[...], adv_lo[...])
    hidden[...] = jnp.tanh(dot3(taps_first, adv_taps))

    got1()
    kz_rows = [recv1[pl.ds(k, 64, stride=2), :] for k in range(2)]
    send2[...] = x_transform(kz_rows, both(ex))
    got2, sent2 = exchange(1, "narrow", 16, send2, recv2)

    got2()
    spectrum = dot3(both(ty), split(swap_blocks(recv2[...])))
    spectrum = project(spectrum, w, n)
    send3[...] = dot3(both(tyi), split(spectrum))
    got3, sent3 = exchange(2, "narrow", 24, send3, recv3)

    got3()
    send4[...] = dot3(both(txi), split(pack_rows(recv3[...])))
    got4, sent4 = exchange(3, "wide", 4, send4, recv4)

    got4()
    for x in range(4):
        big = dot3(split(recv4[pl.ds(x, 64, stride=4), :]), both(zi), (0, 0))
        inner = big[:48, :N] + big[48:96, N:]
        outer = big[96:104, :N] + big[104:112, N:]
        for c in range(3):
            at = 4 * x + c
            proj[at : at + 1] = outer[2 * c : 2 * c + 1]
            proj[pl.ds(16 + at, 16, stride=16), :] = inner[16 * c : 16 * c + 16]
            proj[272 + at : 273 + at] = outer[2 * c + 1 : 2 * c + 2]
            if x in (1, 2):
                proj_own[c, x - 1] = inner[16 * c : 16 * c + 16]

    taps(proj[...], proj_hi, proj_lo)
    proj_taps = (proj_hi[...], proj_lo[...])
    hid = hidden[...]
    pre = split(dot3(taps_second, proj_taps) * (1.0 - hid * hid))
    for kind, (rows, cols) in enumerate(((pre, adv_taps), (split(hid), proj_taps))):
        raw = dot3(rows, cols, (1, 1))
        total = jnp.zeros((16, N), F32)
        for x in range(2):
            for piece in split(raw[16 * x : 16 * x + 16]):
                total = total + dot(piece, gather[kind, x], (1, 0))
        part[16 * kind : 16 * kind + 16] = total
    got5, sent5 = exchange(4, "narrow", 4, part, recv5)

    scattered[...] = dot3(taps_first, pre, (0, 0))
    for y in range(18):
        moved = []
        for dz in range(3):
            total = None
            for dy in range(3):
                if 0 <= y - dy < 16:
                    at = (3 * dy + dz) * 16
                    term = scattered[at : at + 16, N * (y - dy) : N * (y - dy) + N]
                    total = term if total is None else total + term
            moved.append(total if dz == 1 else roll(total, dz - 1))
        gpart[16 * y : 16 * y + 16] = moved[0] + moved[1] + moved[2]
    for x in range(4):
        for c in range(3):
            at = 4 * x + c
            gnat[c, x, 7:8] = gpart[at : at + 1]
            gnat[c, x, 8:24] = gpart[pl.ds(16 + at, 16, stride=16), :]
            gnat[c, x, 24:25] = gpart[272 + at : 273 + at]
    own_x, own_y = pl.ds(1, 2), pl.ds(8, 16)
    first_y, last_y = pl.ds(0, 8), pl.ds(24, 8)
    e1 = copies(
        [
            (gnat.at[:, 0, own_y, :], face_x.at[1], (left, n)),
            (gnat.at[:, 3, own_y, :], face_x.at[0], (right, n)),
            (gnat.at[:, own_x, first_y, :], face_y.at[1], (w, below)),
            (gnat.at[:, own_x, last_y, :], face_y.at[0], (w, above)),
            (gnat.at[:, 0, first_y, :], corner.at[3], (left, below)),
            (gnat.at[:, 0, last_y, :], corner.at[2], (left, above)),
            (gnat.at[:, 3, first_y, :], corner.at[1], (right, below)),
            (gnat.at[:, 3, last_y, :], corner.at[0], (right, above)),
        ],
        e1_send,
        e1_recv,
    )

    got5()

    def fold(value):
        value = jnp.sum(value.reshape(value.shape[0] // 8, 8, N), axis=0)
        return value[0:4] + value[4:8]

    mine[...] = fold(recv5[...])
    got6, sent6 = exchange(5, "wide", 4, mine, recv6)

    for copy in e1:
        copy.wait_recv()
    for c in range(3):
        for x in range(2):
            own = proj_own[c, x] + gnat[c, x + 1, 8:24] + face_x[x, c]
            start = own[0:8] + face_y[0, c, x] + corner[2 * x, c]
            end = own[8:16] + face_y[1, c, x] + corner[2 * x + 1, c]
            gext[c, x + 1, 8:16] = start
            gext[c, x + 1, 16:24] = end
    e2 = copies(
        [
            (gext.at[:, 1, own_y, :], gext.at[:, 3, own_y, :], (left, n)),
            (gext.at[:, 2, own_y, :], gext.at[:, 0, own_y, :], (right, n)),
            (gext.at[:, own_x, pl.ds(8, 8), :], gext.at[:, own_x, last_y, :], (w, below)),
            (gext.at[:, own_x, pl.ds(16, 8), :], gext.at[:, own_x, first_y, :], (w, above)),
        ],
        e2_send,
        e2_recv,
    )
    for copy in e2:
        copy.wait_recv()

    for x in range(2):
        vx, gx = x + 2, x + 1
        v = [vext[c, vx] for c in range(3)]
        g = [gext[c, gx] for c in range(3)]
        positive = [jnp.maximum(a, 0.0) for a in v]
        negative = [jnp.minimum(a, 0.0) for a in v]
        totals = [jnp.zeros((32, N), F32)] * 3
        slopes = []
        for j in range(3):
            slope = jnp.zeros((32, N), F32)
            for c in range(3):
                here = (positive[j] - negative[j]) * g[c]
                if j == 0:
                    ahead = jnp.maximum(vext[0, vx + 1], 0.0) * gext[c, gx + 1]
                    behind = jnp.minimum(vext[0, vx - 1], 0.0) * gext[c, gx - 1]
                    before, after = vext[c, vx - 1], vext[c, vx + 1]
                elif j == 1:
                    ahead = shift_rows(positive[1] * g[c], -1)
                    behind = shift_rows(negative[1] * g[c], 1)
                    before, after = shift_rows(v[c], 1), shift_rows(v[c], -1)
                else:
                    ahead = roll(positive[2] * g[c], -1)
                    behind = roll(negative[2] * g[c], 1)
                    before, after = roll(v[c], 1), roll(v[c], -1)
                totals[c] = totals[c] + here - ahead + behind
                rising, falling = v[c] - before, after - v[c]
                level = 0.5 * (rising + falling)
                slope = slope + g[c] * jnp.where(
                    v[j] > 0.0, rising, jnp.where(v[j] < 0.0, falling, level)
                )
            slopes.append(slope)
        for c in range(3):
            out[c, x] = (g[c] - STEP * totals[c] - STEP * slopes[c])[8:24]

    got6()
    whole[...] = fold(recv6[...]) * (N * N * N) ** -0.5
    got7, sent7 = exchange(6, "narrow", 4, whole, recv7)
    got7()
    sums[...] = recv7[...]

    for sent in (sent1, sent2, sent3, sent4, sent5, sent6, sent7):
        sent()
    for copy in vel_copies + e1 + e2:
        copy.wait_send()


def local(velocity, cotangents, lead_table, lead_index, first_kernel, first_bias, second_kernel):
    first = jnp.concatenate([first_kernel.reshape(16, 81), first_bias[:, None]], axis=1)
    second = jnp.transpose(second_kernel.reshape(3, 16, 27), (1, 0, 2)).reshape(16, 81)
    kcat = jnp.concatenate(
        [jnp.pad(first, ((0, 0), (0, N - 82))), jnp.pad(second, ((0, 0), (0, N - 81)))], axis=0
    )
    constants = [jnp.asarray(t) for t in tables()]

    def v(*shape, kind=F32):
        return pltpu.VMEM(shape, kind)

    dma = pltpu.SemaphoreType.DMA
    in_vmem = pl.BlockSpec(memory_space=pltpu.VMEM)
    in_smem = pl.BlockSpec(memory_space=pltpu.SMEM)
    grad, sums = pl.pallas_call(
        kernel,
        out_shape=(
            jax.ShapeDtypeStruct((3, 2, 16, N), F32),
            jax.ShapeDtypeStruct((32, N), F32),
        ),
        in_specs=[in_vmem, in_vmem, in_smem, in_smem, in_vmem] + [in_vmem] * len(constants),
        out_specs=(in_vmem, in_vmem),
        scratch_shapes=[
            v(128, N), v(128, N), v(128, N), v(128, N), v(192, N), v(192, N), v(256, N), v(256, N),
            v(32, N), v(32, N), v(4, N), v(256, N), v(4, N), v(32, N),
            v(3, 6, 32, N), v(288, N), v(288, N), v(3, 2, 16, N),
            v(144, 2048, kind=BF16), v(144, 2048, kind=BF16),
            v(144, 2048, kind=BF16), v(144, 2048, kind=BF16),
            v(32, 2048), v(144, 2048), v(288, N), v(3, 4, 32, N),
            v(2, 3, 16, N), v(2, 3, 2, 8, N), v(4, 3, 8, N), v(3, 4, 32, N),
            dma((7,)), dma((7,)), dma((7,)), dma((8,)), dma((8,)), dma((8,)), dma((8,)),
            dma((4,)), dma((4,)),
        ],
        compiler_params=pltpu.CompilerParams(
            collective_id=0, has_side_effects=True, vmem_limit_bytes=48 * 1024 * 1024
        ),
        name="step_backward",
    )(cotangents, velocity, lead_table, lead_index, kcat, *constants)
    grad_first = sums[:16, :81].reshape(16, 3, 3, 3, 3)
    grad_bias = sums[:16, 81]
    grad_second = jnp.transpose(sums[16:, :81].reshape(16, 3, 27), (1, 0, 2)).reshape(3, 16, 3, 3, 3)
    return grad, grad_first, grad_bias, grad_second


def solution(mesh):
    placed = (
        P(None, "wide", "narrow", None),
        P(None, None, "wide", "narrow", None),
        P(),
        P(),
        P(),
        P(),
        P(),
    )
    return jax.shard_map(
        local,
        mesh=mesh,
        in_specs=placed,
        out_specs=(P(None, "wide", "narrow", None), P(), P(), P()),
        check_vma=False,
    )
```

```python
import math

import jax
import jax.numpy as jnp
import ml_dtypes
import numpy as np
from jax import lax
from jax.experimental import pallas as pl
from jax.experimental.pallas import tpu as pltpu
from jax.sharding import PartitionSpec as P

F32 = jnp.float32
BF16 = jnp.bfloat16
MESH = pl.DeviceIdType.MESH
N = 128
WIDE = 64
NARROW = 8
STEP = 0.25
BIAS = 108
TABLES = 8


def basis(kind, wave):
    cell = np.arange(N)
    if kind == 0 and wave == 0:
        return np.full(N, 1.0 / math.sqrt(N))
    if kind == 1 and wave == 0:
        return (1.0 - 2.0 * (cell % 2)) / math.sqrt(N)
    angle = 2.0 * np.pi * (cell * wave % N) / N
    return math.sqrt(2.0 / N) * (np.cos(angle) if kind == 0 else np.sin(angle))


def halves(table):
    high = table.astype(np.float32).astype(ml_dtypes.bfloat16)
    low = (table - high.astype(np.float64)).astype(np.float32).astype(ml_dtypes.bfloat16)
    return np.stack([high, low])


def tables():
    tz = np.stack([basis(i % 2, i // 2) for i in range(N)])
    tx = np.stack([basis((i % 16) // 8, 8 * (i // 16) + i % 8) for i in range(N)])
    ty = np.stack([basis(i // 64, i % 64) for i in range(N)])
    ex = np.concatenate([tx[:, 0::2], tx[:, 1::2]], axis=0)
    rows = []
    for n in range(NARROW):
        cells = [16 * n + r for r in range(16)] + [16 * n - 1, 16 * n + 16]
        for y in cells:
            rows.append(ty[:, y % N])
        rows.extend([np.zeros(N)] * 6)
    tyi = np.stack(rows)
    txi = np.stack([tx[:, (2 * w - 1 + x) % N] for w in range(WIDE) for x in range(4)])
    zi = np.stack([tz[0::2], tz[1::2]])
    spread = np.zeros((2, 2, N, 256))
    gather = np.zeros((2, 2, 144, N))
    for x in range(2):
        for c in range(3):
            for dx in range(3):
                for dy in range(3):
                    for dz in range(3):
                        flat = 4 * (c * 9 + dx * 3 + dy) + dz
                        lane = (dy * 3 + dz) * 16 + 4 * (x + dx) + c
                        back = ((2 - dy) * 3 + 2 - dz) * 16 + 4 * (x + 2 - dx) + c
                        spread[0, x, flat, lane] = 1.0
                        spread[1, x, flat, back] = 1.0
                        gather[0, x, lane, flat] = 1.0
                        gather[1, x, back, flat] = 1.0
        spread[0, x, BIAS, 4 * 16 + 3] = 1.0
        gather[0, x, 4 * 16 + 3, BIAS] = 1.0
    exact = ml_dtypes.bfloat16
    return (
        halves(tz),
        halves(ex),
        halves(ty),
        halves(tyi),
        halves(txi),
        halves(zi),
        np.stack([spread[..., :N], spread[..., N:]], axis=2).astype(exact),
        gather.astype(exact),
    )


def split(value):
    high = value.astype(BF16)
    return high, (value - high.astype(F32)).astype(BF16)


def dot(a, b, dims):
    return lax.dot_general(
        a, b, (((dims[0],), (dims[1],)), ((), ())), preferred_element_type=F32
    )


def dot3(a, b, dims=(1, 0)):
    return dot(a[0], b[0], dims) + dot(a[0], b[1], dims) + dot(a[1], b[0], dims)


def both(ref):
    return ref[0], ref[1]


def roll(value, shift):
    return pltpu.roll(value, shift % value.shape[1], 1)


def lanes():
    return lax.broadcasted_iota(jnp.int32, (1, N), 1)


def swap_blocks(m):
    m = m.T
    lane = lanes()
    for bit in (1, 2, 4):
        size = 16 * bit
        odd = (lane // size) % 2 == 1
        parts = []
        for i in range(0, N, 2 * size):
            low, high = m[i : i + size], m[i + size : i + 2 * size]
            parts.append(jnp.where(odd, roll(high, size), low))
            parts.append(jnp.where(odd, high, roll(low, -size)))
        m = jnp.concatenate(parts, axis=0)
    return m


def x_transform(received, ex):
    pair = jnp.concatenate(received, axis=1)
    big = dot3(ex, split(pair))
    lane = lanes()
    first = big[:N, :N] + roll(big[N:, :N], -48)
    second = roll(big[:N, N:], 48) + big[N:, N:]
    return jnp.where(lane < 48, first, jnp.where(lane < 96, second, 0.0))


def project(field, w, n):
    lane = lanes()
    row = lax.broadcasted_iota(jnp.int32, (N, 1), 0)
    block = lane // 16
    comp = block % 3
    is_sin_z = block // 3 % 2 == 1
    slot = lane % 16
    inside = lane < 96
    wave_x = 8 * n + slot % 8
    nyq_x = jnp.logical_and(slot == 8, n == 0)
    nyq_y = row == 64
    nyq_z = jnp.logical_and(is_sin_z, w == 0)
    kx = jnp.where(nyq_x, 64, wave_x).astype(F32)
    ky = jnp.where(nyq_y, 64, row % 64).astype(F32)
    kz = jnp.where(nyq_z, 64, w).astype(F32)
    inverse = 1.0 / jnp.maximum(kx * kx + ky * ky + kz * kz, 1.0)
    dx = jnp.where(slot < 8, wave_x, -wave_x).astype(F32)
    dy = jnp.where(row < 64, row % 64, -(row % 64)).astype(F32)
    dz = jnp.where(is_sin_z, -w, w).astype(F32)
    nyquist = jnp.where(
        comp == 0,
        jnp.where(nyq_x, 64.0, 0.0),
        jnp.where(comp == 2, jnp.where(nyq_z, 64.0, 0.0), 0.0),
    )
    nyquist = nyquist + jnp.where(jnp.logical_and(comp == 1, nyq_y), 64.0, 0.0)

    def derive(v):
        along_x = dx * jnp.where(slot < 8, roll(v, -8), roll(v, 8))
        along_y = dy * jnp.concatenate([v[64:], v[:64]], axis=0)
        along_z = dz * jnp.where(is_sin_z, roll(v, 48), roll(v, -48))
        return jnp.where(comp == 0, along_x, jnp.where(comp == 1, along_y, along_z))

    def over_components(v):
        total = (v + roll(v, -16) + roll(v, -32)) * inverse
        total = jnp.where(jnp.logical_and(inside, comp == 0), total, 0.0)
        return total + roll(total, 16) + roll(total, 32)

    main = over_components(derive(field))
    rest = over_components(nyquist * field)
    return field + derive(main) - nyquist * rest


def pack_rows(received):
    lane = lanes()
    inner = jnp.concatenate([received[24 * i : 24 * i + 16] for i in range(NARROW)], axis=0)
    none = jnp.zeros((8, N), F32)
    outer = []
    for i in range(NARROW):
        outer.extend([received[24 * i + 16 : 24 * i + 24], none])
    inner = swap_blocks(inner)
    outer = swap_blocks(jnp.concatenate(outer, axis=0))
    full = jnp.where(lane < 96, inner, 0.0)
    for k in range(2):
        for c in range(3):
            place = 96 + 8 * k + 2 * c
            here = jnp.logical_and(lane >= place, lane < place + 2)
            full = jnp.where(here, roll(outer, place - 16 * (3 * k + c)), full)
    return full


def taps(field, high_ref, low_ref):
    for dz in range(3):
        moved = field if dz == 1 else roll(field, 1 - dz)
        for ref, part in zip((high_ref, low_ref), split(moved)):
            for dy in range(3):
                at = (3 * dy + dz) * 16
                for y in range(16):
                    ref[at : at + 16, N * y : N * y + N] = part[16 * (y + dy) : 16 * (y + dy) + 16]


def shift_rows(value, by):
    return pltpu.roll(value, by % value.shape[0], 0)


def kernel(
    cot_hbm, vel_hbm, table_hbm, index_hbm, first_hbm, bias_hbm, second_hbm, *refs
):
    tables_hbm, refs = refs[:TABLES], refs[TABLES:]
    (out, sums), refs = refs[:2], refs[2:]
    (cot, table, index, first, bias, second), refs = refs[:6], refs[6:]
    (tz, ex, ty, tyi, txi, zi, spread, gather), refs = refs[:TABLES], refs[TABLES:]
    (
    send1, recv1, send2, recv2, send3, recv3, send4, recv4,
    part, recv5, mine, recv6, whole, recv7,
    vext, adv, proj, proj_own, adv_hi, adv_lo, proj_hi, proj_lo,
    hidden, scattered, gpart, gnat, face_x, face_y, corner, gext,
    flat, own_sem, send_sem, recv_sem, vel_send, vel_recv, e1_send, e1_recv, e2_send, e2_recv,
    load_sem,
    ) = refs
    w = lax.axis_index("wide")
    n = lax.axis_index("narrow")
    wy, wz, wx = w // 16, w // 4 % 4, w % 4
    zl, core = n // 2, n % 2
    right, left = lax.rem(w + 1, WIDE), lax.rem(w + WIDE - 1, WIDE)
    above, below = lax.rem(n + 1, NARROW), lax.rem(n + NARROW - 1, NARROW)

    column = 16 * wy + 4 * wz + zl
    member = 2 * wx + core
    stays = wx == zl

    def each_column(act):
        def body(i, carry):
            j = i // 4
            oz = 8 + jnp.where(j % 2 == 1, (j + 1) // 2, -(j // 2))
            act(lax.rem(wy + 3 - i % 4, 4) * 16 + lax.rem(4 * wz + zl + oz, 16))
            return carry

        lax.fori_loop(0, WIDE - 1, body, 0)

    def each_wide(act):
        for oz in (2, 1, 3, 0):

            def body(i, carry, oz=oz):
                y, x = lax.rem(wy + 3 - i // 4, 4), lax.rem(wx + 3 - i % 4, 4)
                act(y * 16 + lax.rem(wz + oz, 4) * 4 + x)
                return carry

            lax.fori_loop(0, 15 if oz == 0 else 16, body, 0)

    def each_member(act):
        for i in (4, 5, 3, 2, 6, 7, 1):
            act(lax.rem(member + i, NARROW))

    def at_column(p, x):
        return (p // 16 * 16 + p % 16 // 4 * 4 + x, p % 4 * 2 + core)

    outward = (WIDE, each_column, lambda p: at_column(p, zl), column, w, stays)
    inward = (WIDE, each_wide, lambda p: (p, member), w, column, stays)
    columns = (WIDE, each_column, lambda p: at_column(p, wx), column, column, None)
    members = (
        NARROW,
        each_member,
        lambda p: (w - wx + p // 2, n - core + p % 2),
        member,
        member,
        None,
    )

    barrier = pltpu.get_barrier_semaphore()

    def greet(device):
        pl.semaphore_signal(barrier, inc=1, device_id=device, device_id_type=MESH)

    each_wide(lambda p: greet((p, member)))

    @pl.when(jnp.logical_not(stays))
    def _():
        greet((w, member))

    each_member(lambda p: greet(members[2](p)))
    neighbours = (
        (right, n), (left, n), (w, above), (w, below),
        (right, above), (right, below), (left, above), (left, below),
    )
    for device in neighbours:
        greet(device)

    loads = [
        pltpu.make_async_copy(source, target, load_sem.at[i])
        for i, (source, target) in enumerate(
            [
                (cot_hbm, cot),
                (table_hbm, table),
                (index_hbm, index),
                (tables_hbm[0], tz),
                (vel_hbm, vext.at[:, pl.ds(2, 2), pl.ds(8, 16), :]),
                (first_hbm, first),
                (bias_hbm, bias),
                (second_hbm, second),
            ]
            + list(zip(tables_hbm[1:], (ex, ty, tyi, txi, zi, spread, gather)))
        )
    ]
    for load in loads:
        load.start()

    for load in loads[:4]:
        load.wait()
    weight = [table[index[l]] for l in range(4)]
    pieces = []
    for x in range(2):
        for c in range(3):
            total = weight[0] * cot[0, c, x]
            for l in range(1, 4):
                total = total + weight[l] * cot[l, c, x]
            pieces.append(total)
    pieces.append(jnp.zeros((32, N), F32))
    combined = jnp.concatenate(pieces, axis=0)
    send1[...] = dot3(both(tz), split(combined), (1, 1))

    for load in loads[4:]:
        load.wait()

    taps_first, taps_second = [], []
    for kind, (ref, place) in enumerate(((first, taps_first), (second, taps_second))):
        flat[...] = jnp.zeros_like(flat)
        for tap in range(27):
            flat[4 * tap : 4 * tap + 3, 0:16] = ref[tap // 9, tap // 3 % 3, tap % 3]
        if kind == 0:
            flat[BIAS : BIAS + 1, 0:16] = bias[...]
        for piece in split(flat[...]):
            rows = []
            for x in range(2):
                cols = [dot(piece, spread[kind, x, i], (0, 0))[:16] for i in range(2)]
                rows.append(jnp.concatenate(cols, axis=1)[:, :144])
            place.append(jnp.concatenate(rows, axis=0).astype(BF16))

    proj[...] = jnp.zeros_like(proj)
    face_y[...] = jnp.zeros_like(face_y)
    corner[...] = jnp.zeros_like(corner)
    sublane = lax.broadcasted_iota(jnp.int32, (288, N), 0) % 16
    adv[...] = jnp.where(sublane == 3, 1.0, 0.0)

    pl.semaphore_wait(barrier, WIDE + NARROW + 6 + jnp.where(stays, 0, 1))
    pending = []

    def copies(moves, sends, recvs):
        made = []
        for i, (source, target, device) in enumerate(moves):
            made.append(
                pltpu.make_async_remote_copy(
                    source, target, sends.at[i], recvs.at[i], device_id=device, device_id_type=MESH
                )
            )
        for copy in made:
            copy.start()
            pending.append(copy.wait_send)
        return made

    def exchange(i, group, rows, source, target):
        size, each, device, own, slot, kept = group

        def block(ref, p):
            return ref.at[pl.ds(p * rows, rows)]

        def piece(p):
            return source if source.shape[0] == rows else block(source, p)

        def copy(a, b, to):
            return pltpu.make_async_remote_copy(
                a, b, send_sem.at[i], recv_sem.at[i], device_id=to, device_id_type=MESH
            )

        def act(p):
            copy(piece(p), block(target, slot), device(p)).start()

        each(act)
        keep = pltpu.make_async_copy(piece(own), block(target, slot), own_sem.at[i])
        some = target.at[pl.ds(0, (size - 1) * rows)]
        others = copy(some, some, (right, n))
        if kept is None:
            keep.start()
            pending.append(others.wait_send)

            def arrived():
                keep.wait()
                others.wait_recv()

            return arrived
        everyone = copy(target, target, (right, n))

        def either(here, there):
            pl.when(kept)(here)
            pl.when(jnp.logical_not(kept))(there)

        either(lambda: keep.start(), lambda: act(own))
        pending.append(lambda: either(lambda: others.wait_send(), lambda: everyone.wait_send()))

        def arrived():
            def here():
                keep.wait()
                others.wait_recv()

            either(here, lambda: everyone.wait_recv())

        return arrived

    got1 = exchange(0, outward, 2, send1, recv1)

    got1()
    kz_rows = [recv1[pl.ds(k, 64, stride=2), :] for k in range(2)]
    send2[...] = x_transform(kz_rows, both(ex))
    got2 = exchange(1, members, 16, send2, recv2)

    low, high, full = pl.ds(8, 2), pl.ds(22, 2), pl.ds(8, 16)
    moves = []
    for device, rows, xs, ys in zip(
        neighbours,
        (full, full, high, low, high, low, high, low),
        (0, 4, 2, 2, 0, 0, 4, 4),
        (full, full, pl.ds(6, 2), pl.ds(24, 2)) + (pl.ds(6, 2), pl.ds(24, 2)) * 2,
    ):
        source = vext.at[:, pl.ds(2, 2), rows, :]
        moves.append((source, vext.at[:, pl.ds(xs, 2), ys, :], device))
    vel_copies = copies(moves, vel_send, vel_recv)

    got2()
    spectrum = dot3(both(ty), split(swap_blocks(recv2[...])))
    spectrum = project(spectrum, column, member)
    send3[...] = dot3(both(tyi), split(spectrum))
    got3 = exchange(2, members, 24, send3, recv3)

    got3()
    send4[...] = dot3(both(txi), split(pack_rows(recv3[...])))
    got4 = exchange(3, inward, 4, send4, recv4)

    for copy in vel_copies:
        copy.wait_recv()
    for x in range(4):
        v = [vext[c, x + 1] for c in range(3)]
        totals = [jnp.zeros((32, N), F32)] * 3
        for j in range(3):
            positive, negative = jnp.maximum(v[j], 0.0), jnp.minimum(v[j], 0.0)
            for c in range(3):
                if j == 0:
                    before, after = vext[c, x], vext[c, x + 2]
                elif j == 1:
                    before, after = shift_rows(v[c], 1), shift_rows(v[c], -1)
                else:
                    before, after = roll(v[c], 1), roll(v[c], -1)
                totals[c] = totals[c] + positive * (v[c] - before) + negative * (after - v[c])
        for c in range(3):
            done = v[c] - STEP * totals[c]
            at = 4 * x + c
            adv[at : at + 1] = done[7:8]
            adv[pl.ds(16 + at, 16, stride=16), :] = done[8:24]
            adv[272 + at : 273 + at] = done[24:25]
    taps(adv[...], adv_hi, adv_lo)
    adv_taps = (adv_hi[...], adv_lo[...])
    hidden[...] = jnp.tanh(dot3(taps_first, adv_taps))

    got4()
    for x in range(4):
        rows = split(recv4[pl.ds(x, 64, stride=4), :])
        even, odd = (dot3(rows, (zi[0, k], zi[1, k]), (0, 0)) for k in range(2))
        inner = even[:48] + odd[48:96]
        outer = even[96:104] + odd[104:112]
        for c in range(3):
            at = 4 * x + c
            proj[at : at + 1] = outer[2 * c : 2 * c + 1]
            proj[pl.ds(16 + at, 16, stride=16), :] = inner[16 * c : 16 * c + 16]
            proj[272 + at : 273 + at] = outer[2 * c + 1 : 2 * c + 2]
            if x in (1, 2):
                proj_own[c, x - 1] = inner[16 * c : 16 * c + 16]

    taps(proj[...], proj_hi, proj_lo)
    proj_taps = (proj_hi[...], proj_lo[...])
    hid = hidden[...]
    pre = split(dot3(taps_second, proj_taps) * (1.0 - hid * hid))

    scattered[...] = dot3(taps_first, pre, (0, 0))
    for y in range(18):
        moved = []
        for dz in range(3):
            total = None
            for dy in range(3):
                if 0 <= y - dy < 16:
                    at = (3 * dy + dz) * 16
                    term = scattered[at : at + 16, N * (y - dy) : N * (y - dy) + N]
                    total = term if total is None else total + term
            moved.append(total if dz == 1 else roll(total, dz - 1))
        gpart[16 * y : 16 * y + 16] = moved[0] + moved[1] + moved[2]
    for x in range(4):
        for c in range(3):
            at = 4 * x + c
            gnat[c, x, 7:8] = gpart[at : at + 1]
            gnat[c, x, 8:24] = gpart[pl.ds(16 + at, 16, stride=16), :]
            gnat[c, x, 24:25] = gpart[272 + at : 273 + at]
    own_x, own_y = pl.ds(1, 2), pl.ds(8, 16)
    row_0, row_7, row_8, row_23, row_24 = (pl.ds(r, 1) for r in (0, 7, 8, 23, 24))
    e1 = copies(
        [
            (gnat.at[:, 3, own_y, :], face_x.at[0], (right, n)),
            (gnat.at[:, 0, own_y, :], face_x.at[1], (left, n)),
            (gnat.at[:, own_x, row_24, :], face_y.at[0, :, :, row_0, :], (w, above)),
            (gnat.at[:, own_x, row_7, :], face_y.at[1, :, :, row_7, :], (w, below)),
            (gnat.at[:, 3, row_24, :], corner.at[0, :, row_0, :], (right, above)),
            (gnat.at[:, 3, row_7, :], corner.at[1, :, row_7, :], (right, below)),
            (gnat.at[:, 0, row_24, :], corner.at[2, :, row_0, :], (left, above)),
            (gnat.at[:, 0, row_7, :], corner.at[3, :, row_7, :], (left, below)),
        ],
        e1_send,
        e1_recv,
    )

    for kind, (rows, cols) in enumerate(((pre, adv_taps), (split(hid), proj_taps))):
        raw = dot3(rows, cols, (1, 1))
        total = jnp.zeros((16, N), F32)
        for x in range(2):
            for piece in split(raw[16 * x : 16 * x + 16]):
                total = total + dot(piece, gather[kind, x], (1, 0))
        part[16 * kind : 16 * kind + 16] = total
    got5 = exchange(4, members, 4, part, recv5)

    got5()

    def fold(value):
        value = jnp.sum(value.reshape(value.shape[0] // 8, 8, N), axis=0)
        return value[0:4] + value[4:8]

    mine[...] = fold(recv5[...])
    got6 = exchange(5, columns, 4, mine, recv6)

    for copy in e1:
        copy.wait_recv()
    for c in range(3):
        for x in range(2):
            own = proj_own[c, x] + gnat[c, x + 1, 8:24] + face_x[x, c]
            start = own[0:8] + face_y[0, c, x] + corner[2 * x, c]
            end = own[8:16] + face_y[1, c, x] + corner[2 * x + 1, c]
            gext[c, x + 1, 8:16] = start
            gext[c, x + 1, 16:24] = end
    e2 = copies(
        [
            (gext.at[:, 1, own_y, :], gext.at[:, 3, own_y, :], (left, n)),
            (gext.at[:, 2, own_y, :], gext.at[:, 0, own_y, :], (right, n)),
            (gext.at[:, own_x, row_8, :], gext.at[:, own_x, row_24, :], (w, below)),
            (gext.at[:, own_x, row_23, :], gext.at[:, own_x, row_7, :], (w, above)),
        ],
        e2_send,
        e2_recv,
    )
    got6()
    whole[...] = fold(recv6[...]) * (N * N * N) ** -0.5
    got7 = exchange(6, members, 4, whole, recv7)

    for copy in e2:
        copy.wait_recv()

    for x in range(2):
        vx, gx = x + 2, x + 1
        v = [vext[c, vx] for c in range(3)]
        g = [gext[c, gx] for c in range(3)]
        positive = [jnp.maximum(a, 0.0) for a in v]
        negative = [jnp.minimum(a, 0.0) for a in v]
        totals = [jnp.zeros((32, N), F32)] * 3
        slopes = []
        for j in range(3):
            slope = jnp.zeros((32, N), F32)
            for c in range(3):
                here = (positive[j] - negative[j]) * g[c]
                if j == 0:
                    ahead = jnp.maximum(vext[0, vx + 1], 0.0) * gext[c, gx + 1]
                    behind = jnp.minimum(vext[0, vx - 1], 0.0) * gext[c, gx - 1]
                    before, after = vext[c, vx - 1], vext[c, vx + 1]
                elif j == 1:
                    ahead = shift_rows(positive[1] * g[c], -1)
                    behind = shift_rows(negative[1] * g[c], 1)
                    before, after = shift_rows(v[c], 1), shift_rows(v[c], -1)
                else:
                    ahead = roll(positive[2] * g[c], -1)
                    behind = roll(negative[2] * g[c], 1)
                    before, after = roll(v[c], 1), roll(v[c], -1)
                totals[c] = totals[c] + here - ahead + behind
                rising, falling = v[c] - before, after - v[c]
                level = 0.5 * (rising + falling)
                slope = slope + g[c] * jnp.where(
                    v[j] > 0.0, rising, jnp.where(v[j] < 0.0, falling, level)
                )
            slopes.append(slope)
        for c in range(3):
            out[c, x] = (g[c] - STEP * totals[c] - STEP * slopes[c])[8:24]

    got7()
    sums[...] = recv7[...]

    for wait in pending:
        wait()


def hand_out(grad, sums, out, out_first, out_bias, out_second):
    out[...] = grad[...]
    for kind, ref in enumerate((out_first, out_second)):
        turned = sums[16 * kind : 16 * kind + 16].T
        for tap in range(27):
            ref[tap // 9, tap // 3 % 3, tap % 3] = turned[4 * tap : 4 * tap + 3]
        if kind == 0:
            out_bias[...] = turned[BIAS : BIAS + 1]


def local(velocity, cotangents, lead_table, lead_index, first_kernel, first_bias, second_kernel):
    constants = tables()

    def v(*shape, kind=F32):
        return pltpu.VMEM(shape, kind)

    dma = pltpu.SemaphoreType.DMA
    in_vmem = pl.BlockSpec(memory_space=pltpu.VMEM)
    anywhere = pl.BlockSpec(memory_space=pl.ANY)
    shapes = tuple(
        jax.ShapeDtypeStruct(shape, F32)
        for shape in ((3, 2, 16, N), (3, 3, 3, 3, 16), (1, 16), (3, 3, 3, 3, 16))
    )
    results = pl.pallas_call(
        kernel,
        out_shape=(shapes[0], jax.ShapeDtypeStruct((32, N), F32)),
        in_specs=[anywhere] * (7 + TABLES),
        out_specs=(in_vmem,) * 2,
        scratch_shapes=[
            v(4, 3, 2, 16, N), pltpu.SMEM((8,), F32), pltpu.SMEM((4,), jnp.int32),
            v(3, 3, 3, 3, 16), v(1, 16), v(3, 3, 3, 3, 16),
            *[v(*t.shape, kind=BF16) for t in constants],
            v(128, N), v(128, N), v(128, N), v(128, N), v(192, N), v(192, N), v(256, N), v(256, N),
            v(32, N), v(32, N), v(4, N), v(256, N), v(4, N), v(32, N),
            v(3, 6, 32, N), v(288, N), v(288, N), v(3, 2, 16, N),
            v(144, 2048, kind=BF16), v(144, 2048, kind=BF16),
            v(144, 2048, kind=BF16), v(144, 2048, kind=BF16),
            v(32, 2048), v(144, 2048), v(288, N), v(3, 4, 32, N),
            v(2, 3, 16, N), v(2, 3, 2, 8, N), v(4, 3, 8, N), v(3, 4, 32, N),
            v(N, N), dma((7,)), dma((7,)), dma((7,)), dma((8,)), dma((8,)), dma((8,)), dma((8,)),
            dma((4,)), dma((4,)), dma((7 + TABLES,)),
        ],
        compiler_params=pltpu.CompilerParams(
            collective_id=0, has_side_effects=True, vmem_limit_bytes=60 * 1024 * 1024
        ),
        name="step_backward",
    )(
        cotangents, velocity, lead_table, lead_index,
        jnp.transpose(first_kernel, (1, 2, 3, 4, 0)), first_bias[None],
        jnp.transpose(second_kernel, (0, 2, 3, 4, 1)), *[jnp.asarray(t) for t in constants],
    )
    grad, first, bias, second = pl.pallas_call(
        hand_out,
        out_shape=shapes,
        in_specs=[in_vmem] * 2,
        out_specs=(in_vmem,) * 4,
        name="hand_out",
    )(*results)
    return (
        grad,
        jnp.transpose(first, (4, 0, 1, 2, 3)),
        bias[0],
        jnp.transpose(second, (0, 4, 1, 2, 3)),
    )


def solution(mesh):
    placed = (
        P(None, "wide", "narrow", None),
        P(None, None, "wide", "narrow", None),
        P(),
        P(),
        P(),
        P(),
        P(),
    )
    return jax.shard_map(
        local,
        mesh=mesh,
        in_specs=placed,
        out_specs=(P(None, "wide", "narrow", None), P(), P(), P()),
        check_vma=False,
    )
```

```python
import math

import jax
import jax.numpy as jnp
import ml_dtypes
import numpy as np
from jax import lax
from jax.experimental import pallas as pl
from jax.experimental.pallas import tpu as pltpu
from jax.sharding import PartitionSpec as P

F32 = jnp.float32
BF16 = jnp.bfloat16
MESH = pl.DeviceIdType.MESH
N = 128
WIDE = 64
NARROW = 8
STEP = 0.25
BIAS = 108
TABLES = 8


def basis(kind, wave):
    cell = np.arange(N)
    if kind == 0 and wave == 0:
        return np.full(N, 1.0 / math.sqrt(N))
    if kind == 1 and wave == 0:
        return (1.0 - 2.0 * (cell % 2)) / math.sqrt(N)
    angle = 2.0 * np.pi * (cell * wave % N) / N
    return math.sqrt(2.0 / N) * (np.cos(angle) if kind == 0 else np.sin(angle))


def halves(table):
    high = table.astype(np.float32).astype(ml_dtypes.bfloat16)
    low = (table - high.astype(np.float64)).astype(np.float32).astype(ml_dtypes.bfloat16)
    return high, low


def left_factor(table):
    high, low = halves(table)
    return np.stack([high, low, high])


def tables():
    tz = np.stack([basis(i % 2, i // 2) for i in range(N)])
    tx = np.stack([basis((i % 16) // 8, 8 * (i // 16) + i % 8) for i in range(N)])
    ty = np.stack([basis(i // 64, i % 64) for i in range(N)])
    ex = np.concatenate([tx[:, 0::2], tx[:, 1::2]], axis=0)
    rows = []
    for n in range(NARROW):
        cells = [16 * n + r for r in range(16)] + [16 * n - 1, 16 * n + 16]
        for y in cells:
            rows.append(ty[:, y % N])
        rows.extend([np.zeros(N)] * 6)
    tyi = np.stack(rows)
    txi = np.stack([tx[:, (2 * w - 1 + x) % N] for w in range(WIDE) for x in range(4)])
    zi = np.stack([tz[0::2], tz[1::2]])
    spread = np.zeros((2, 2, N, 256))
    gather = np.zeros((2, 2, 144, N))
    for x in range(2):
        for c in range(3):
            for dx in range(3):
                for dy in range(3):
                    for dz in range(3):
                        tap = c * 27 + dx * 9 + dy * 3 + dz
                        flat = 4 * (tap // 3) + tap % 3
                        lane = (dy * 3 + dz) * 16 + 4 * (x + dx) + c
                        back = ((2 - dy) * 3 + 2 - dz) * 16 + 4 * (x + 2 - dx) + c
                        spread[0, x, flat, lane] = 1.0
                        spread[1, x, flat, back] = 1.0
                        gather[0, x, lane, tap] = 1.0
                        gather[1, x, back, tap] = 1.0
        spread[0, x, BIAS, 4 * 16 + 3] = 1.0
        gather[0, x, 4 * 16 + 3, 81] = 1.0
    exact = ml_dtypes.bfloat16
    return (
        left_factor(tz),
        np.stack([np.concatenate(halves(ex), axis=1), np.pad(halves(ex)[0], ((0, 0), (0, 64)))]),
        left_factor(ty),
        left_factor(tyi),
        left_factor(txi),
        np.stack([np.concatenate([h, h, l]) for h, l in map(halves, zi)]),
        np.stack([spread[..., :N], spread[..., N:]], axis=2).astype(exact),
        gather.astype(exact),
    )


def split(value):
    high = value.astype(BF16)
    return high, (value - high.astype(F32)).astype(BF16)


def dot(a, b, dims):
    return lax.dot_general(
        a, b, (((dims[0],), (dims[1],)), ((), ())), preferred_element_type=F32
    )


def left(ref):
    return jnp.concatenate([ref[i] for i in range(ref.shape[0])], axis=1)


def right(value, axis=0):
    high, low = split(value)
    return jnp.concatenate([high, high, low], axis=axis)


def stacked(pair, other, dims):
    rows = pair[0].shape[0]
    both = dot(jnp.concatenate(pair, axis=0), other[0], dims)
    return both[:rows] + both[rows:] + dot(pair[0], other[1], dims)


def roll(value, shift):
    return pltpu.roll(value, shift % value.shape[1], 1)


def lanes():
    return lax.broadcasted_iota(jnp.int32, (1, N), 1)


def swap_blocks(m):
    m = m.T
    lane = lanes()
    for bit in (1, 2, 4):
        size = 16 * bit
        odd = (lane // size) % 2 == 1
        parts = []
        for i in range(0, N, 2 * size):
            low, high = m[i : i + size], m[i + size : i + 2 * size]
            parts.append(jnp.where(odd, roll(high, size), low))
            parts.append(jnp.where(odd, high, roll(low, -size)))
        m = jnp.concatenate(parts, axis=0)
    return m


def x_transform(received, ex):
    high, low = split(jnp.concatenate(received, axis=1))
    big = dot(ex, jnp.concatenate([high, high, low, jnp.zeros_like(low)], axis=0), (1, 0))
    lane = lanes()
    first = big[:N, :N] + roll(big[N:, :N], -48)
    second = roll(big[:N, N:], 48) + big[N:, N:]
    return jnp.where(lane < 48, first, jnp.where(lane < 96, second, 0.0))


def project(field, w, n):
    lane = lanes()
    row = lax.broadcasted_iota(jnp.int32, (N, 1), 0)
    block = lane // 16
    comp = block % 3
    is_sin_z = block // 3 % 2 == 1
    slot = lane % 16
    inside = lane < 96
    wave_x = 8 * n + slot % 8
    nyq_x = jnp.logical_and(slot == 8, n == 0)
    nyq_y = row == 64
    nyq_z = jnp.logical_and(is_sin_z, w == 0)
    kx = jnp.where(nyq_x, 64, wave_x).astype(F32)
    ky = jnp.where(nyq_y, 64, row % 64).astype(F32)
    kz = jnp.where(nyq_z, 64, w).astype(F32)
    inverse = 1.0 / jnp.maximum(kx * kx + ky * ky + kz * kz, 1.0)
    dx = jnp.where(slot < 8, wave_x, -wave_x).astype(F32)
    dy = jnp.where(row < 64, row % 64, -(row % 64)).astype(F32)
    dz = jnp.where(is_sin_z, -w, w).astype(F32)
    nyquist = jnp.where(
        comp == 0,
        jnp.where(nyq_x, 64.0, 0.0),
        jnp.where(comp == 2, jnp.where(nyq_z, 64.0, 0.0), 0.0),
    )
    nyquist = nyquist + jnp.where(jnp.logical_and(comp == 1, nyq_y), 64.0, 0.0)

    def derive(v):
        along_x = dx * jnp.where(slot < 8, roll(v, -8), roll(v, 8))
        along_y = dy * jnp.concatenate([v[64:], v[:64]], axis=0)
        along_z = dz * jnp.where(is_sin_z, roll(v, 48), roll(v, -48))
        return jnp.where(comp == 0, along_x, jnp.where(comp == 1, along_y, along_z))

    def over_components(v):
        total = (v + roll(v, -16) + roll(v, -32)) * inverse
        total = jnp.where(jnp.logical_and(inside, comp == 0), total, 0.0)
        return total + roll(total, 16) + roll(total, 32)

    main = over_components(derive(field))
    rest = over_components(nyquist * field)
    return field + derive(main) - nyquist * rest


def pack_rows(received):
    lane = lanes()
    inner = jnp.concatenate([received[24 * i : 24 * i + 16] for i in range(NARROW)], axis=0)
    none = jnp.zeros((8, N), F32)
    outer = []
    for i in range(NARROW):
        outer.extend([received[24 * i + 16 : 24 * i + 24], none])
    inner = swap_blocks(inner)
    outer = swap_blocks(jnp.concatenate(outer, axis=0))
    full = jnp.where(lane < 96, inner, 0.0)
    for k in range(2):
        for c in range(3):
            place = 96 + 8 * k + 2 * c
            here = jnp.logical_and(lane >= place, lane < place + 2)
            full = jnp.where(here, roll(outer, place - 16 * (3 * k + c)), full)
    return full


def taps(field, high_ref, low_ref):
    for dz in range(3):
        moved = field if dz == 1 else roll(field, 1 - dz)
        for ref, part in zip((high_ref, low_ref), split(moved)):
            for dy in range(3):
                at = (3 * dy + dz) * 16
                for y in range(16):
                    ref[at : at + 16, N * y : N * y + N] = part[16 * (y + dy) : 16 * (y + dy) + 16]


def shift_rows(value, by):
    return pltpu.roll(value, by % value.shape[0], 0)


def kernel(
    cot_hbm, vel_hbm, table_hbm, index_hbm, first_hbm, bias_hbm, second_hbm, *refs
):
    tables_hbm, refs = refs[:TABLES], refs[TABLES:]
    (out_hbm, sums_hbm), refs = refs[:2], refs[2:]
    (cot, table, index, first, bias, second), refs = refs[:6], refs[6:]
    (tz, ex, ty, tyi, txi, zi, spread, gather), refs = refs[:TABLES], refs[TABLES:]
    (
    send1, recv1, send2, recv2, send3, recv3, send4, recv4,
    part, recv5, mine, recv6, whole, out,
    vext, adv, proj, proj_own, adv_hi, adv_lo, proj_hi, proj_lo,
    hidden, hid_hi, hid_lo, scattered, gpart, gnat, face_x, face_y, corner, gext,
    flat, own_sem, send_sem, recv_sem, vel_send, vel_recv, e1_send, e1_recv, e2_send, e2_recv,
    load_sem,
    ) = refs
    w = lax.axis_index("wide")
    n = lax.axis_index("narrow")
    wy, wz, wx = w // 16, w // 4 % 4, w % 4
    zl, core = n // 2, n % 2
    ahead_w, behind_w = lax.rem(w + 1, WIDE), lax.rem(w + WIDE - 1, WIDE)
    above, below = lax.rem(n + 1, NARROW), lax.rem(n + NARROW - 1, NARROW)

    far = lax.rem(n + 4, NARROW)
    longer = jnp.where(zl < 2, 1, 3)

    def each_wide(act):
        def offset(i):
            return jnp.where(i < 2, 2 + i, 3 - i)

        for pair in ((2, longer), (0, lax.rem(longer + 2, 4))):
            zs = [lax.rem(wz + oz, 4) * 4 for oz in pair]

            def body(i, carry, zs=zs):
                place = lax.rem(wy + offset(i // 4), 4) * 16 + lax.rem(wx + offset(i % 4), 4)
                for z in zs:
                    act(place + z)
                return carry

            lax.fori_loop(0, 16, body, 0)

    def each_narrow(act):
        for i in (4, 5, 3, 2, 6, 7, 1):
            act(lax.rem(far + i, NARROW))

    member = 2 * wx + core
    column = 16 * wy + 4 * wz + zl

    def each_member(act):
        for i in (4, 5, 3, 2, 6, 7, 1):
            act(lax.rem(member + i, NARROW))

    def each_column(act):
        def body(i, carry):
            j = i // 4
            oz = 8 + jnp.where(j % 2 == 1, (j + 1) // 2, -(j // 2))
            act(lax.rem(wy + 3 - i % 4, 4) * 16 + lax.rem(4 * wz + zl + oz, 16))
            return carry

        lax.fori_loop(0, WIDE - 1, body, 0)

    across = (WIDE, each_wide, lambda p: (p, far), None, w)
    narrow = (NARROW, each_narrow, lambda p: (w, lax.rem(p + 4, NARROW)), far, far)
    members = (
        NARROW,
        each_member,
        lambda p: (w - wx + p // 2, n - core + p % 2),
        member,
        member,
    )
    columns = (
        WIDE,
        each_column,
        lambda p: (p // 16 * 16 + p % 16 // 4 * 4 + wx, p % 4 * 2 + core),
        column,
        column,
    )

    barrier = pltpu.get_barrier_semaphore()

    def greet(device):
        pl.semaphore_signal(barrier, inc=1, device_id=device, device_id_type=MESH)

    each_wide(lambda p: greet((p, far)))
    neighbours = (
        (ahead_w, n), (behind_w, n), (w, above), (w, below),
        (ahead_w, above), (ahead_w, below), (behind_w, above), (behind_w, below),
    )
    for i in (5, 3, 2, 6, 7, 1):
        greet((w, lax.rem(n + i, NARROW)))
    for device in neighbours[:2] + neighbours[4:]:
        greet(device)

    loads = [
        pltpu.make_async_copy(source, target, load_sem.at[i])
        for i, (source, target) in enumerate(
            [
                (cot_hbm, cot),
                (table_hbm, table),
                (index_hbm, index),
                (tables_hbm[0], tz),
                (vel_hbm, vext.at[:, pl.ds(2, 2), pl.ds(8, 16), :]),
                (first_hbm, first),
                (bias_hbm, bias),
                (second_hbm, second),
            ]
            + list(zip(tables_hbm[1:], (ex, ty, tyi, txi, zi, spread, gather)))
        )
    ]
    for load in loads:
        load.start()

    for load in loads[:4]:
        load.wait()
    weight = [table[index[l]] for l in range(4)]
    pieces = []
    for x in range(2):
        for c in range(3):
            total = weight[0] * cot[0, c, x]
            for l in range(1, 4):
                total = total + weight[l] * cot[l, c, x]
            pieces.append(total)
    pieces.append(jnp.zeros((32, N), F32))
    combined = jnp.concatenate(pieces, axis=0)
    send1[...] = dot(left(tz), right(combined, 1), (1, 1))

    for load in loads[4:]:
        load.wait()

    pl.semaphore_wait(barrier, WIDE + 12)
    pending = []

    def copies(moves, sends, recvs):
        made = []
        for i, (source, target, device) in enumerate(moves):
            made.append(
                pltpu.make_async_remote_copy(
                    source, target, sends.at[i], recvs.at[i], device_id=device, device_id_type=MESH
                )
            )
        for copy in made:
            copy.start()
            pending.append(copy.wait_send)
        return made

    def exchange(i, group, rows, source, target):
        size, each, device, own, slot = group

        def block(ref, p):
            return ref.at[pl.ds(p * rows, rows)]

        def piece(p):
            return source if source.shape[0] == rows else block(source, p)

        def copy(a, b, to):
            return pltpu.make_async_remote_copy(
                a, b, send_sem.at[i], recv_sem.at[i], device_id=to, device_id_type=MESH
            )

        each(lambda p: copy(piece(p), block(target, slot), device(p)).start())
        some = target if own is None else target.at[pl.ds(0, (size - 1) * rows)]
        others = copy(some, some, (w, far))
        pending.append(others.wait_send)
        if own is None:
            return others.wait_recv
        keep = pltpu.make_async_copy(piece(own), block(target, slot), own_sem.at[i])
        keep.start()

        def arrived():
            keep.wait()
            others.wait_recv()

        return arrived

    got1 = exchange(0, across, 2, send1, recv1)

    low, high, full = pl.ds(8, 2), pl.ds(22, 2), pl.ds(8, 16)
    moves = []
    for device, rows, xs, ys in zip(
        neighbours,
        (full, full, high, low, high, low, high, low),
        (0, 4, 2, 2, 0, 0, 4, 4),
        (full, full, pl.ds(6, 2), pl.ds(24, 2)) + (pl.ds(6, 2), pl.ds(24, 2)) * 2,
    ):
        source = vext.at[:, pl.ds(2, 2), rows, :]
        moves.append((source, vext.at[:, pl.ds(xs, 2), ys, :], device))
    vel_copies = copies(moves, vel_send, vel_recv)

    taps_first, taps_second = [], []
    for kind, (ref, place) in enumerate(((first, taps_first), (second, taps_second))):
        flat[...] = jnp.zeros_like(flat)
        for tap in range(27):
            flat[4 * tap : 4 * tap + 3, 0:16] = ref[tap // 9, tap // 3 % 3, tap % 3]
        if kind == 0:
            flat[BIAS : BIAS + 1, 0:16] = bias[...]
        for piece in split(flat[...]):
            rows = []
            for x in range(2):
                cols = [dot(piece, spread[kind, x, i], (0, 0))[:16] for i in range(2)]
                rows.append(jnp.concatenate(cols, axis=1)[:, :144])
            place.append(jnp.concatenate(rows, axis=0).astype(BF16))

    proj[...] = jnp.zeros_like(proj)
    face_y[...] = jnp.zeros_like(face_y)
    corner[...] = jnp.zeros_like(corner)
    sublane = lax.broadcasted_iota(jnp.int32, (288, N), 0) % 16
    adv[...] = jnp.where(sublane == 3, 1.0, 0.0)

    got1()
    kz_rows = [recv1[pl.ds(k, 64, stride=2), :] for k in range(2)]
    send2[...] = x_transform(kz_rows, left(ex))
    got2 = exchange(1, narrow, 16, send2, recv2)

    got2()
    spectrum = dot(left(ty), right(swap_blocks(recv2[...])), (1, 0))
    spectrum = project(spectrum, w, far)
    send3[...] = dot(left(tyi), right(spectrum), (1, 0))
    got3 = exchange(2, narrow, 24, send3, recv3)

    got3()
    send4[...] = dot(left(txi), right(pack_rows(recv3[...])), (1, 0))
    got4 = exchange(3, across, 4, send4, recv4)

    for copy in vel_copies:
        copy.wait_recv()
    for x in range(4):
        v = [vext[c, x + 1] for c in range(3)]
        totals = [jnp.zeros((32, N), F32)] * 3
        for j in range(3):
            positive, negative = jnp.maximum(v[j], 0.0), jnp.minimum(v[j], 0.0)
            for c in range(3):
                if j == 0:
                    before, after = vext[c, x], vext[c, x + 2]
                elif j == 1:
                    before, after = shift_rows(v[c], 1), shift_rows(v[c], -1)
                else:
                    before, after = roll(v[c], 1), roll(v[c], -1)
                totals[c] = totals[c] + positive * (v[c] - before) + negative * (after - v[c])
        for c in range(3):
            done = v[c] - STEP * totals[c]
            at = 4 * x + c
            adv[at : at + 1] = done[7:8]
            adv[pl.ds(16 + at, 16, stride=16), :] = done[8:24]
            adv[272 + at : 273 + at] = done[24:25]
    taps(adv[...], adv_hi, adv_lo)
    adv_taps = (adv_hi[...], adv_lo[...])
    hid = jnp.tanh(stacked(taps_first, adv_taps, (1, 0)))
    hidden[...] = 1.0 - hid * hid
    hid_hi[...], hid_lo[...] = split(hid)

    got4()
    high, low = split(jnp.concatenate([recv4[pl.ds(x, 64, stride=4), :] for x in range(4)], axis=1))
    fields = dot(jnp.concatenate([high, low, high], axis=0), left(zi), (0, 0))
    for x in range(4):
        even, odd = fields[N * x : N * x + N, :N], fields[N * x : N * x + N, N:]
        inner = even[:48] + odd[48:96]
        outer = even[96:104] + odd[104:112]
        for c in range(3):
            at = 4 * x + c
            proj[at : at + 1] = outer[2 * c : 2 * c + 1]
            proj[pl.ds(16 + at, 16, stride=16), :] = inner[16 * c : 16 * c + 16]
            proj[272 + at : 273 + at] = outer[2 * c + 1 : 2 * c + 2]
            if x in (1, 2):
                proj_own[c, x - 1] = inner[16 * c : 16 * c + 16]

    taps(proj[...], proj_hi, proj_lo)
    proj_taps = (proj_hi[...], proj_lo[...])
    pre = split(stacked(taps_second, proj_taps, (1, 0)) * hidden[...])

    gradients = []
    for kind, (rows, cols) in enumerate(((pre, adv_taps), ((hid_hi[...], hid_lo[...]), proj_taps))):
        raw = stacked(rows, cols, (1, 1))
        total = jnp.zeros((16, N), F32)
        for x in range(2):
            for piece in split(raw[16 * x : 16 * x + 16]):
                total = total + dot(piece, gather[kind, x], (1, 0))
        gradients.append(total)
    lane = lanes()
    beside = jnp.logical_and(lane >= 82, lane < 123)
    spare = gradients[1][8:]
    part[0:8] = jnp.where(beside, roll(spare, 82), gradients[0][:8])
    part[8:16] = jnp.where(beside, roll(spare, 41), gradients[0][8:])
    part[16:24] = gradients[1][:8]
    got5 = exchange(4, members, 3, part, recv5)

    scattered[...] = dot(
        jnp.concatenate([*taps_first, taps_first[0]], axis=0),
        jnp.concatenate([pre[0], pre[0], pre[1]], axis=0),
        (0, 0),
    )
    for y in range(18):
        moved = []
        for dz in range(3):
            total = None
            for dy in range(3):
                if 0 <= y - dy < 16:
                    at = (3 * dy + dz) * 16
                    term = scattered[at : at + 16, N * (y - dy) : N * (y - dy) + N]
                    total = term if total is None else total + term
            moved.append(total if dz == 1 else roll(total, dz - 1))
        gpart[16 * y : 16 * y + 16] = moved[0] + moved[1] + moved[2]
    for x in range(4):
        for c in range(3):
            at = 4 * x + c
            gnat[c, x, 7:8] = gpart[at : at + 1]
            gnat[c, x, 8:24] = gpart[pl.ds(16 + at, 16, stride=16), :]
            gnat[c, x, 24:25] = gpart[272 + at : 273 + at]
    own_x, own_y = pl.ds(1, 2), pl.ds(8, 16)
    row_0, row_7, row_8, row_23, row_24 = (pl.ds(r, 1) for r in (0, 7, 8, 23, 24))
    e1 = copies(
        [
            (gnat.at[:, 3, own_y, :], face_x.at[0], (ahead_w, n)),
            (gnat.at[:, 0, own_y, :], face_x.at[1], (behind_w, n)),
            (gnat.at[:, own_x, row_24, :], face_y.at[0, :, :, row_0, :], (w, above)),
            (gnat.at[:, own_x, row_7, :], face_y.at[1, :, :, row_7, :], (w, below)),
            (gnat.at[:, 3, row_24, :], corner.at[0, :, row_0, :], (ahead_w, above)),
            (gnat.at[:, 3, row_7, :], corner.at[1, :, row_7, :], (ahead_w, below)),
            (gnat.at[:, 0, row_24, :], corner.at[2, :, row_0, :], (behind_w, above)),
            (gnat.at[:, 0, row_7, :], corner.at[3, :, row_7, :], (behind_w, below)),
        ],
        e1_send,
        e1_recv,
    )

    got5()

    def fold(ref):
        count = ref.shape[0] // 3
        return [
            jnp.sum(ref[pl.ds(row, count, stride=3), :], axis=0, keepdims=True) for row in range(3)
        ]

    for row, total in enumerate(fold(recv5)):
        mine[row : row + 1] = total
    got6 = exchange(5, columns, 3, mine, recv6)

    for copy in e1:
        copy.wait_recv()
    for c in range(3):
        for x in range(2):
            own = proj_own[c, x] + gnat[c, x + 1, 8:24] + face_x[x, c]
            start = own[0:8] + face_y[0, c, x] + corner[2 * x, c]
            end = own[8:16] + face_y[1, c, x] + corner[2 * x + 1, c]
            gext[c, x + 1, 8:16] = start
            gext[c, x + 1, 16:24] = end
    e2 = copies(
        [
            (gext.at[:, 1, own_y, :], gext.at[:, 3, own_y, :], (behind_w, n)),
            (gext.at[:, 2, own_y, :], gext.at[:, 0, own_y, :], (ahead_w, n)),
            (gext.at[:, own_x, row_8, :], gext.at[:, own_x, row_24, :], (w, below)),
            (gext.at[:, own_x, row_23, :], gext.at[:, own_x, row_7, :], (w, above)),
        ],
        e2_send,
        e2_recv,
    )
    got6()
    for row, total in enumerate(fold(recv6)):
        whole[row : row + 1] = total * (N * N * N) ** -0.5
    got7 = exchange(6, members, 3, whole, sums_hbm)

    for copy in e2:
        copy.wait_recv()

    for x in range(2):
        vx, gx = x + 2, x + 1
        v = [vext[c, vx] for c in range(3)]
        g = [gext[c, gx] for c in range(3)]
        positive = [jnp.maximum(a, 0.0) for a in v]
        negative = [jnp.minimum(a, 0.0) for a in v]
        totals = [jnp.zeros((32, N), F32)] * 3
        slopes = []
        for j in range(3):
            slope = jnp.zeros((32, N), F32)
            for c in range(3):
                here = (positive[j] - negative[j]) * g[c]
                if j == 0:
                    ahead = jnp.maximum(vext[0, vx + 1], 0.0) * gext[c, gx + 1]
                    behind = jnp.minimum(vext[0, vx - 1], 0.0) * gext[c, gx - 1]
                    before, after = vext[c, vx - 1], vext[c, vx + 1]
                elif j == 1:
                    ahead = shift_rows(positive[1] * g[c], -1)
                    behind = shift_rows(negative[1] * g[c], 1)
                    before, after = shift_rows(v[c], 1), shift_rows(v[c], -1)
                else:
                    ahead = roll(positive[2] * g[c], -1)
                    behind = roll(negative[2] * g[c], 1)
                    before, after = roll(v[c], 1), roll(v[c], -1)
                totals[c] = totals[c] + here - ahead + behind
                rising, falling = v[c] - before, after - v[c]
                level = 0.5 * (rising + falling)
                slope = slope + g[c] * jnp.where(
                    v[j] > 0.0, rising, jnp.where(v[j] < 0.0, falling, level)
                )
            slopes.append(slope)
        for c in range(3):
            out[c, x] = (g[c] - STEP * totals[c] - STEP * slopes[c])[8:24]

    store = pltpu.make_async_copy(out, out_hbm, load_sem.at[7 + TABLES])
    store.start()
    got7()
    store.wait()
    for wait in pending:
        wait()


def hand_out(grad, sums, out, out_first, out_bias, out_second):
    out[...] = grad[...]
    lane = lanes()
    spare = jnp.where(lane < 41, roll(sums[0:8], -82), roll(sums[8:16], -41))
    both = (sums[0:16], jnp.concatenate([sums[16:24], spare], axis=0))
    for kind, ref in enumerate((out_first, out_second)):
        turned = both[kind].T
        for tap in range(27):
            ref[tap // 9, tap // 3 % 3, tap % 3] = turned[3 * tap : 3 * tap + 3]
        if kind == 0:
            out_bias[...] = turned[81:82]


def local(velocity, cotangents, lead_table, lead_index, first_kernel, first_bias, second_kernel):
    constants = tables()

    def v(*shape, kind=F32):
        return pltpu.VMEM(shape, kind)

    dma = pltpu.SemaphoreType.DMA
    in_vmem = pl.BlockSpec(memory_space=pltpu.VMEM)
    anywhere = pl.BlockSpec(memory_space=pl.ANY)
    shapes = tuple(
        jax.ShapeDtypeStruct(shape, F32)
        for shape in ((3, 2, 16, N), (3, 3, 3, 3, 16), (1, 16), (3, 3, 3, 3, 16))
    )
    results = pl.pallas_call(
        kernel,
        out_shape=(shapes[0], jax.ShapeDtypeStruct((24, N), F32)),
        in_specs=[anywhere] * (7 + TABLES),
        out_specs=(anywhere,) * 2,
        scratch_shapes=[
            v(4, 3, 2, 16, N), pltpu.SMEM((8,), F32), pltpu.SMEM((4,), jnp.int32),
            v(3, 3, 3, 3, 16), v(1, 16), v(3, 3, 3, 3, 16),
            *[v(*t.shape, kind=BF16) for t in constants],
            v(128, N), v(128, N), v(128, N), v(128, N), v(192, N), v(192, N), v(256, N), v(256, N),
            v(24, N), v(24, N), v(3, N), v(192, N), v(3, N), v(3, 2, 16, N),
            v(3, 6, 32, N), v(288, N), v(288, N), v(3, 2, 16, N),
            v(144, 2048, kind=BF16), v(144, 2048, kind=BF16),
            v(144, 2048, kind=BF16), v(144, 2048, kind=BF16),
            v(32, 2048), v(32, 2048, kind=BF16), v(32, 2048, kind=BF16),
            v(144, 2048), v(288, N), v(3, 4, 32, N),
            v(2, 3, 16, N), v(2, 3, 2, 8, N), v(4, 3, 8, N), v(3, 4, 32, N),
            v(N, N), dma((7,)), dma((7,)), dma((7,)), dma((8,)), dma((8,)), dma((8,)), dma((8,)),
            dma((4,)), dma((4,)), dma((8 + TABLES,)),
        ],
        compiler_params=pltpu.CompilerParams(
            collective_id=0, has_side_effects=True, vmem_limit_bytes=60 * 1024 * 1024
        ),
        name="step_backward",
    )(
        cotangents, velocity, lead_table, lead_index,
        jnp.transpose(first_kernel, (1, 2, 3, 4, 0)), first_bias[None],
        jnp.transpose(second_kernel, (0, 2, 3, 4, 1)), *[jnp.asarray(t) for t in constants],
    )
    grad, first, bias, second = pl.pallas_call(
        hand_out,
        out_shape=shapes,
        in_specs=[in_vmem] * 2,
        out_specs=(in_vmem,) * 4,
        name="hand_out",
    )(*results)
    return (
        grad,
        jnp.transpose(first, (4, 0, 1, 2, 3)),
        bias[0],
        jnp.transpose(second, (0, 4, 1, 2, 3)),
    )


def solution(mesh):
    placed = (
        P(None, "wide", "narrow", None),
        P(None, None, "wide", "narrow", None),
        P(),
        P(),
        P(),
        P(),
        P(),
    )
    return jax.shard_map(
        local,
        mesh=mesh,
        in_specs=placed,
        out_specs=(P(None, "wide", "narrow", None), P(), P(), P()),
        check_vma=False,
    )
```

```python
import math

import jax
import jax.numpy as jnp
import ml_dtypes
import numpy as np
from jax import lax
from jax.experimental import pallas as pl
from jax.experimental.pallas import tpu as pltpu
from jax.sharding import PartitionSpec as P

F32 = jnp.float32
BF16 = jnp.bfloat16
MESH = pl.DeviceIdType.MESH
N = 128
WIDE = 64
NARROW = 8
STEP = 0.25
BIAS = 108
TABLES = 7
ORDER = (2, 0, 1)


def basis(kind, wave):
    cell = np.arange(N)
    if kind == 0 and wave == 0:
        return np.full(N, 1.0 / math.sqrt(N))
    if kind == 1 and wave == 0:
        return (1.0 - 2.0 * (cell % 2)) / math.sqrt(N)
    angle = 2.0 * np.pi * (cell * wave % N) / N
    return math.sqrt(2.0 / N) * (np.cos(angle) if kind == 0 else np.sin(angle))


def halves(table):
    high = table.astype(np.float32).astype(ml_dtypes.bfloat16)
    low = (table - high.astype(np.float64)).astype(np.float32).astype(ml_dtypes.bfloat16)
    return high, low


def left_factor(table):
    high, low = halves(table)
    return np.stack([high, low, high])


def thin_factor(table):
    high, low = halves(table)
    return np.stack([np.concatenate([high, low], axis=1), np.pad(high, ((0, 0), (0, 64)))])


def tables():
    tz = np.stack([basis((i % 16) // 8, 8 * (i // 16) + i % 8) for i in range(N)])
    ty = np.stack([basis(i % 2, i // 2) for i in range(N)])
    tx = np.stack([basis(i // 64, i % 64) for i in range(N)])
    ex = np.concatenate([tx[:, 0::2], tx[:, 1::2]], axis=0)
    txi = np.stack([tx[:, (2 * w - 1 + x) % N] for x in range(4) for w in range(WIDE)])
    cells = []
    for n in range(NARROW):
        cells += [16 * n + r for r in range(16)] + [16 * n - 1, 16 * n + 16] + [0] * 6
    tyi = np.concatenate([ty[k::2, np.array(cells) % N].T for k in range(2)], axis=0)
    spread = np.zeros((2, 2, N, 256))
    gather = np.zeros((2, 2, 144, N))
    for x in range(2):
        for c in range(3):
            for dx in range(3):
                for dy in range(3):
                    for dz in range(3):
                        tap = c * 27 + dx * 9 + dy * 3 + dz
                        flat = 4 * (tap // 3) + tap % 3
                        lane = (dy * 3 + dz) * 16 + 4 * (x + dx) + c
                        back = ((2 - dy) * 3 + 2 - dz) * 16 + 4 * (x + 2 - dx) + c
                        spread[0, x, flat, lane] = 1.0
                        spread[1, x, flat, back] = 1.0
                        gather[0, x, lane, tap] = 1.0
                        gather[1, x, back, tap] = 1.0
        spread[0, x, BIAS, 4 * 16 + 3] = 1.0
        gather[0, x, 4 * 16 + 3, 81] = 1.0
    exact = ml_dtypes.bfloat16
    return (
        left_factor(tz),
        left_factor(ty),
        thin_factor(ex),
        left_factor(txi),
        thin_factor(tyi),
        np.stack([spread[..., :N], spread[..., N:]], axis=2).astype(exact),
        gather.astype(exact),
    )


def split(value):
    high = value.astype(BF16)
    return high, (value - high.astype(F32)).astype(BF16)


def dot(a, b, dims):
    return lax.dot_general(
        a, b, (((dims[0],), (dims[1],)), ((), ())), preferred_element_type=F32
    )


def left(ref):
    return jnp.concatenate([ref[i] for i in range(ref.shape[0])], axis=1)


def right(value, axis=0):
    high, low = split(value)
    return jnp.concatenate([high, high, low], axis=axis)


def stacked(pair, other, dims):
    rows = pair[0].shape[0]
    both = dot(jnp.concatenate(pair, axis=0), other[0], dims)
    return both[:rows] + both[rows:] + dot(pair[0], other[1], dims)


def roll(value, shift):
    return pltpu.roll(value, shift % value.shape[1], 1)


def lanes():
    return lax.broadcasted_iota(jnp.int32, (1, N), 1)


def swap_blocks(m):
    lane = lanes()
    for bit in (1, 2, 4):
        size = 16 * bit
        odd = (lane // size) % 2 == 1
        parts = []
        for i in range(0, N, 2 * size):
            low, high = m[i : i + size], m[i + size : i + 2 * size]
            parts.append(jnp.where(odd, roll(high, size), low))
            parts.append(jnp.where(odd, high, roll(low, -size)))
        m = jnp.concatenate(parts, axis=0)
    return m


def thin(table, value):
    high, low = split(value)
    return dot(table, jnp.concatenate([high, high, low, jnp.zeros_like(low)], axis=0), (1, 0))


def from_pairs(even, odd, first, second):
    lane = lanes()
    one = even[:, first] + roll(odd[:, first], -48)
    two = roll(even[:, second], 48) + odd[:, second]
    return jnp.where(lane < 48, one, jnp.where(lane < 96, two, 0.0))


def project(field, w, n):
    lane = lanes()
    row = lax.broadcasted_iota(jnp.int32, (N, 1), 0)
    block = lane // 16
    comp = block % 3
    is_sin_z = block // 3 % 2 == 1
    slot = lane % 16
    inside = lane < 96
    wave_x = 8 * n + slot % 8
    nyq_x = jnp.logical_and(slot == 8, n == 0)
    nyq_y = row == 64
    nyq_z = jnp.logical_and(is_sin_z, w == 0)
    kx = jnp.where(nyq_x, 64, wave_x).astype(F32)
    ky = jnp.where(nyq_y, 64, row % 64).astype(F32)
    kz = jnp.where(nyq_z, 64, w).astype(F32)
    inverse = 1.0 / jnp.maximum(kx * kx + ky * ky + kz * kz, 1.0)
    dx = jnp.where(slot < 8, wave_x, -wave_x).astype(F32)
    dy = jnp.where(row < 64, row % 64, -(row % 64)).astype(F32)
    dz = jnp.where(is_sin_z, -w, w).astype(F32)
    nyquist = jnp.where(
        comp == 0,
        jnp.where(nyq_x, 64.0, 0.0),
        jnp.where(comp == 2, jnp.where(nyq_z, 64.0, 0.0), 0.0),
    )
    nyquist = nyquist + jnp.where(jnp.logical_and(comp == 1, nyq_y), 64.0, 0.0)

    def derive(v):
        along_x = dx * jnp.where(slot < 8, roll(v, -8), roll(v, 8))
        along_y = dy * jnp.concatenate([v[64:], v[:64]], axis=0)
        along_z = dz * jnp.where(is_sin_z, roll(v, 48), roll(v, -48))
        return jnp.where(comp == 0, along_x, jnp.where(comp == 1, along_y, along_z))

    def over_components(v):
        total = (v + roll(v, -16) + roll(v, -32)) * inverse
        total = jnp.where(jnp.logical_and(inside, comp == 0), total, 0.0)
        return total + roll(total, 16) + roll(total, 32)

    main = over_components(derive(field))
    rest = over_components(nyquist * field)
    return field + derive(main) - nyquist * rest


def z_blocks(received, tile):
    rows = [48 * n + 24 * tile for n in range(NARROW)]
    inner = swap_blocks(jnp.concatenate([received[r : r + 16] for r in rows], axis=0))
    none = jnp.zeros((8, N), F32)
    outer = [piece for r in rows for piece in (received[r + 16 : r + 24], none)]
    outer = swap_blocks(jnp.concatenate(outer, axis=0))
    return inner[:96], [outer[16 * b : 16 * b + 8] for b in range(6)]


def taps(field, high_ref, low_ref):
    for dz in range(3):
        moved = field if dz == 1 else roll(field, 1 - dz)
        for ref, part in zip((high_ref, low_ref), split(moved)):
            for dy in range(3):
                at = (3 * dy + dz) * 16
                for y in range(16):
                    ref[at : at + 16, N * y : N * y + N] = part[16 * (y + dy) : 16 * (y + dy) + 16]


def shift_rows(value, by):
    return pltpu.roll(value, by % value.shape[0], 0)


def kernel(
    cot_hbm, vel_hbm, table_hbm, index_hbm, first_hbm, bias_hbm, second_hbm, *refs
):
    tables_hbm, refs = refs[:TABLES], refs[TABLES:]
    (out_hbm, sums_hbm), refs = refs[:2], refs[2:]
    (cot, table, index, first, bias, second), refs = refs[:6], refs[6:]
    (tz, ty, ex, txi, tyi, spread, gather), refs = refs[:TABLES], refs[TABLES:]
    (
    send1, recv1, send2, recv2, send3, recv3, send4, recv4,
    part, recv5, mine, recv6, whole, out,
    vext, adv, proj, proj_own, adv_hi, adv_lo, proj_hi, proj_lo,
    hidden, hid_hi, hid_lo, scattered, gpart, gnat, face_x, face_y, corner, gext,
    flat, own_sem, send_sem, recv_sem, vel_send, vel_recv, e1_send, e1_recv, e2_send, e2_recv,
    load_sem, token,
    ) = refs
    w = lax.axis_index("wide")
    n = lax.axis_index("narrow")
    wy, wz, wx = w // 16, w // 4 % 4, w % 4
    zl, core = n // 2, n % 2
    ahead_w, behind_w = lax.rem(w + 1, WIDE), lax.rem(w + WIDE - 1, WIDE)
    above, below = lax.rem(n + 1, NARROW), lax.rem(n + NARROW - 1, NARROW)

    far = lax.rem(n + 4, NARROW)
    longer = jnp.where(zl < 2, 1, 3)

    def each_wide(act):
        def offset(i):
            return jnp.where(i < 2, 2 + i, 3 - i)

        for pair in ((2, longer), (0, lax.rem(longer + 2, 4))):
            zs = [lax.rem(wz + oz, 4) * 4 for oz in pair]

            def body(i, carry, zs=zs):
                place = lax.rem(wy + offset(i // 4), 4) * 16 + lax.rem(wx + offset(i % 4), 4)
                for z in zs:
                    act(place + z)
                return carry

            lax.fori_loop(0, 16, body, 0)

    def each_plane(act):
        def body(i, carry):
            act(lax.rem(wy + i // 4, 4) * 16 + wz * 4 + lax.rem(wx + i % 4, 4))
            return carry

        lax.fori_loop(1, 16, body, 0)

    def each_narrow(act):
        for i in (4, 5, 3, 2, 6, 7, 1):
            act(lax.rem(n + i, NARROW))

    member = 2 * wx + core
    column = 16 * wy + 4 * wz + zl

    def each_member(act):
        for i in (4, 5, 3, 2, 6, 7, 1):
            act(lax.rem(member + i, NARROW))

    def each_column(act):
        def body(i, carry):
            j = i // 4
            oz = 8 + jnp.where(j % 2 == 1, (j + 1) // 2, -(j // 2))
            act(lax.rem(wy + 3 - i % 4, 4) * 16 + lax.rem(4 * wz + zl + oz, 16))
            return carry

        lax.fori_loop(0, WIDE - 1, body, 0)

    across = (WIDE, each_wide, lambda p: (p, far), None, w)
    narrow = (NARROW, each_narrow, lambda p: (w, p), n, n)
    members = (
        NARROW,
        each_member,
        lambda p: (w - wx + p // 2, n - core + p % 2),
        member,
        member,
    )
    columns = (
        WIDE,
        each_column,
        lambda p: (p // 16 * 16 + p % 16 // 4 * 4 + wx, p % 4 * 2 + core),
        column,
        column,
    )

    barrier = pltpu.get_barrier_semaphore()

    def greet(device):
        pl.semaphore_signal(barrier, inc=1, device_id=device, device_id_type=MESH)

    for i in (2, 1, 3):
        greet((16 * wy + 4 * lax.rem(wz + i, 4) + wx, far))
    each_plane(lambda p: greet((p, n)))
    neighbours = (
        (ahead_w, n), (behind_w, n), (w, above), (w, below),
        (ahead_w, above), (ahead_w, below), (behind_w, above), (behind_w, below),
    )
    each_narrow(lambda p: greet((w, p)))
    for device in neighbours[:2] + neighbours[4:]:
        greet(device)

    loads = [
        pltpu.make_async_copy(source, target, load_sem.at[i])
        for i, (source, target) in enumerate(
            [
                (cot_hbm, cot),
                (table_hbm, table),
                (index_hbm, index),
                (tables_hbm[0], tz),
                (vel_hbm, vext.at[:, pl.ds(2, 2), pl.ds(8, 16), :]),
                (first_hbm, first),
                (bias_hbm, bias),
                (second_hbm, second),
            ]
            + list(zip(tables_hbm[1:], (ty, ex, txi, tyi, spread, gather)))
        )
    ]
    for load in loads:
        load.start()

    for load in loads[:4]:
        load.wait()
    weight = [table[index[l]] for l in range(4)]
    pieces = []
    for x in range(2):
        for c in ORDER:
            total = weight[0] * cot[0, c, x]
            for l in range(1, 4):
                total = total + weight[l] * cot[l, c, x]
            pieces.append(total)
    pieces.append(jnp.zeros((32, N), F32))
    combined = jnp.concatenate(pieces, axis=0)
    send1[...] = dot(left(tz), right(combined, 1), (1, 1))

    for load in loads[4:]:
        load.wait()

    pl.semaphore_wait(barrier, 3 + 15 + 7 + 6)
    pending = []

    def copies(moves, sends, recvs):
        made = []
        for i, (source, target, device) in enumerate(moves):
            made.append(
                pltpu.make_async_remote_copy(
                    source, target, sends.at[i], recvs.at[i], device_id=device, device_id_type=MESH
                )
            )
        for copy in made:
            copy.start()
            pending.append(copy.wait_send)
        return made

    def exchange(i, group, rows, source, target, used=None):
        size, each, device, own, slot = group

        def block(ref, p):
            return ref.at[pl.ds(p * rows, used or rows)]

        def piece(p):
            return source if source.shape[0] == rows else block(source, p)

        def copy(a, b, to):
            return pltpu.make_async_remote_copy(
                a, b, send_sem.at[i], recv_sem.at[i], device_id=to, device_id_type=MESH
            )

        each(lambda p: copy(piece(p), block(target, slot), device(p)).start())
        some = target if own is None else target.at[pl.ds(0, (size - 1) * (used or rows))]
        others = copy(some, some, (w, far))
        pending.append(others.wait_send)
        if own is None:
            return others.wait_recv
        keep = pltpu.make_async_copy(piece(own), block(target, slot), own_sem.at[i])
        keep.start()

        def arrived():
            keep.wait()
            others.wait_recv()

        return arrived

    got1 = exchange(0, narrow, 16, send1, recv1)

    def tell(p):
        pl.semaphore_signal(token, inc=1, device_id=(p, n), device_id_type=MESH)

    each_plane(tell)

    got1()
    send2[...] = dot(left(ty), right(swap_blocks(recv1[...].T)), (1, 0))
    pl.semaphore_wait(token, 15)
    got2 = exchange(1, across, 2, send2, recv2)

    low, high, full = pl.ds(8, 2), pl.ds(22, 2), pl.ds(8, 16)
    moves = []
    for device, rows, xs, ys in zip(
        neighbours,
        (full, full, high, low, high, low, high, low),
        (0, 4, 2, 2, 0, 0, 4, 4),
        (full, full, pl.ds(6, 2), pl.ds(24, 2)) + (pl.ds(6, 2), pl.ds(24, 2)) * 2,
    ):
        source = vext.at[:, pl.ds(2, 2), rows, :]
        moves.append((source, vext.at[:, pl.ds(xs, 2), ys, :], device))
    vel_copies = copies(moves, vel_send, vel_recv)

    taps_first, taps_second = [], []
    for kind, (ref, place) in enumerate(((first, taps_first), (second, taps_second))):
        flat[...] = jnp.zeros_like(flat)
        for tap in range(27):
            flat[4 * tap : 4 * tap + 3, 0:16] = ref[tap // 9, tap // 3 % 3, tap % 3]
        if kind == 0:
            flat[BIAS : BIAS + 1, 0:16] = bias[...]
        for piece in split(flat[...]):
            rows = []
            for x in range(2):
                cols = [dot(piece, spread[kind, x, i], (0, 0))[:16] for i in range(2)]
                rows.append(jnp.concatenate(cols, axis=1)[:, :144])
            place.append(jnp.concatenate(rows, axis=0).astype(BF16))

    proj[...] = jnp.zeros_like(proj)
    face_y[...] = jnp.zeros_like(face_y)
    corner[...] = jnp.zeros_like(corner)
    sublane = lax.broadcasted_iota(jnp.int32, (288, N), 0) % 16
    adv[...] = jnp.where(sublane == 3, 1.0, 0.0)

    got2()
    pair = jnp.concatenate([recv2[pl.ds(k, 64, stride=2), :] for k in range(2)], axis=1)
    field = thin(left(ex), pair)
    first_half, second_half = slice(0, N), slice(N, 2 * N)
    spectrum = project(from_pairs(field[:N], field[N:], first_half, second_half), w, far)
    fields = dot(left(txi), right(spectrum), (1, 0))
    lane = lanes()
    last = fields[192:256]
    for x in range(3):
        rows = jnp.where(lane < 96, fields[64 * x : 64 * x + 64], roll(last, 96 - 32 * x))
        send3[pl.ds(x, 64, stride=3), :] = rows
    got3 = exchange(2, across, 3, send3, recv3)

    for copy in vel_copies:
        copy.wait_recv()
    for x in range(4):
        v = [vext[c, x + 1] for c in range(3)]
        totals = [jnp.zeros((32, N), F32)] * 3
        for j in range(3):
            positive, negative = jnp.maximum(v[j], 0.0), jnp.minimum(v[j], 0.0)
            for c in range(3):
                if j == 0:
                    before, after = vext[c, x], vext[c, x + 2]
                elif j == 1:
                    before, after = shift_rows(v[c], 1), shift_rows(v[c], -1)
                else:
                    before, after = roll(v[c], 1), roll(v[c], -1)
                totals[c] = totals[c] + positive * (v[c] - before) + negative * (after - v[c])
        for c in range(3):
            done = v[c] - STEP * totals[c]
            at = 4 * x + c
            adv[at : at + 1] = done[7:8]
            adv[pl.ds(16 + at, 16, stride=16), :] = done[8:24]
            adv[272 + at : 273 + at] = done[24:25]
    taps(adv[...], adv_hi, adv_lo)
    adv_taps = (adv_hi[...], adv_lo[...])
    hid = jnp.tanh(stacked(taps_first, adv_taps, (1, 0)))
    hidden[...] = 1.0 - hid * hid
    hid_hi[...], hid_lo[...] = split(hid)

    got3()
    rows = [recv3[pl.ds(x, 64, stride=3), :] for x in range(3)]
    rows.append(
        jnp.where(lane < 32, roll(rows[0], 32), jnp.where(lane < 64, roll(rows[1], 64), roll(rows[2], 96)))
    )
    field = thin(left(tyi), jnp.concatenate(rows, axis=1))
    for tile in range(2):
        columns_of = [slice(N * x, N * x + N) for x in (2 * tile, 2 * tile + 1)]
        pieces = from_pairs(field[:192], field[192:], *columns_of)
        for i in range(NARROW):
            send4[48 * i + 24 * tile : 48 * i + 24 * tile + 24] = pieces[24 * i : 24 * i + 24]
    got4 = exchange(3, narrow, 48, send4, recv4, 42)

    got4()
    inner_rows, outer_rows = [], []
    for tile in range(2):
        inner, outer = z_blocks(recv4[...], tile)
        inner_rows.append(inner)
        outer_rows.extend(outer)
    spectra = right(jnp.concatenate(inner_rows + outer_rows, axis=0), 1)
    fields = dot(spectra, jnp.concatenate([tz[i] for i in range(3)], axis=0), (1, 0))
    for x in range(4):
        for place, c in enumerate(ORDER):
            block = 3 * x + place
            inner = fields[16 * block : 16 * block + 16]
            outer = fields[192 + 8 * block : 192 + 8 * block + 8]
            at = 4 * x + c
            proj[at : at + 1] = outer[0:1]
            proj[pl.ds(16 + at, 16, stride=16), :] = inner
            proj[272 + at : 273 + at] = outer[1:2]
            if x in (1, 2):
                proj_own[c, x - 1] = inner

    taps(proj[...], proj_hi, proj_lo)
    proj_taps = (proj_hi[...], proj_lo[...])
    pre = split(stacked(taps_second, proj_taps, (1, 0)) * hidden[...])

    gradients = []
    for kind, (rows, cols) in enumerate(((pre, adv_taps), ((hid_hi[...], hid_lo[...]), proj_taps))):
        raw = stacked(rows, cols, (1, 1))
        total = jnp.zeros((16, N), F32)
        for x in range(2):
            for piece in split(raw[16 * x : 16 * x + 16]):
                total = total + dot(piece, gather[kind, x], (1, 0))
        gradients.append(total)
    lane = lanes()
    beside = jnp.logical_and(lane >= 82, lane < 123)
    spare = gradients[1][8:]
    part[0:8] = jnp.where(beside, roll(spare, 82), gradients[0][:8])
    part[8:16] = jnp.where(beside, roll(spare, 41), gradients[0][8:])
    part[16:24] = gradients[1][:8]
    got5 = exchange(4, members, 3, part, recv5)

    scattered[...] = dot(
        jnp.concatenate([*taps_first, taps_first[0]], axis=0),
        jnp.concatenate([pre[0], pre[0], pre[1]], axis=0),
        (0, 0),
    )
    for y in range(18):
        moved = []
        for dz in range(3):
            total = None
            for dy in range(3):
                if 0 <= y - dy < 16:
                    at = (3 * dy + dz) * 16
                    term = scattered[at : at + 16, N * (y - dy) : N * (y - dy) + N]
                    total = term if total is None else total + term
            moved.append(total if dz == 1 else roll(total, dz - 1))
        gpart[16 * y : 16 * y + 16] = moved[0] + moved[1] + moved[2]
    for x in range(4):
        for c in range(3):
            at = 4 * x + c
            gnat[c, x, 7:8] = gpart[at : at + 1]
            gnat[c, x, 8:24] = gpart[pl.ds(16 + at, 16, stride=16), :]
            gnat[c, x, 24:25] = gpart[272 + at : 273 + at]
    own_x, own_y = pl.ds(1, 2), pl.ds(8, 16)
    row_0, row_7, row_8, row_23, row_24 = (pl.ds(r, 1) for r in (0, 7, 8, 23, 24))
    e1 = copies(
        [
            (gnat.at[:, 3, own_y, :], face_x.at[0], (ahead_w, n)),
            (gnat.at[:, 0, own_y, :], face_x.at[1], (behind_w, n)),
            (gnat.at[:, own_x, row_24, :], face_y.at[0, :, :, row_0, :], (w, above)),
            (gnat.at[:, own_x, row_7, :], face_y.at[1, :, :, row_7, :], (w, below)),
            (gnat.at[:, 3, row_24, :], corner.at[0, :, row_0, :], (ahead_w, above)),
            (gnat.at[:, 3, row_7, :], corner.at[1, :, row_7, :], (ahead_w, below)),
            (gnat.at[:, 0, row_24, :], corner.at[2, :, row_0, :], (behind_w, above)),
            (gnat.at[:, 0, row_7, :], corner.at[3, :, row_7, :], (behind_w, below)),
        ],
        e1_send,
        e1_recv,
    )

    got5()

    def fold(ref):
        count = ref.shape[0] // 3
        return [
            jnp.sum(ref[pl.ds(row, count, stride=3), :], axis=0, keepdims=True) for row in range(3)
        ]

    for row, total in enumerate(fold(recv5)):
        mine[row : row + 1] = total
    got6 = exchange(5, columns, 3, mine, recv6)

    for copy in e1:
        copy.wait_recv()
    for c in range(3):
        for x in range(2):
            own = proj_own[c, x] + gnat[c, x + 1, 8:24] + face_x[x, c]
            start = own[0:8] + face_y[0, c, x] + corner[2 * x, c]
            end = own[8:16] + face_y[1, c, x] + corner[2 * x + 1, c]
            gext[c, x + 1, 8:16] = start
            gext[c, x + 1, 16:24] = end
    e2 = copies(
        [
            (gext.at[:, 1, own_y, :], gext.at[:, 3, own_y, :], (behind_w, n)),
            (gext.at[:, 2, own_y, :], gext.at[:, 0, own_y, :], (ahead_w, n)),
            (gext.at[:, own_x, row_8, :], gext.at[:, own_x, row_24, :], (w, below)),
            (gext.at[:, own_x, row_23, :], gext.at[:, own_x, row_7, :], (w, above)),
        ],
        e2_send,
        e2_recv,
    )
    got6()
    for row, total in enumerate(fold(recv6)):
        whole[row : row + 1] = total * (N * N * N) ** -0.5
    got7 = exchange(6, members, 3, whole, sums_hbm)

    for copy in e2:
        copy.wait_recv()

    for x in range(2):
        vx, gx = x + 2, x + 1
        v = [vext[c, vx] for c in range(3)]
        g = [gext[c, gx] for c in range(3)]
        positive = [jnp.maximum(a, 0.0) for a in v]
        negative = [jnp.minimum(a, 0.0) for a in v]
        totals = [jnp.zeros((32, N), F32)] * 3
        slopes = []
        for j in range(3):
            slope = jnp.zeros((32, N), F32)
            for c in range(3):
                here = (positive[j] - negative[j]) * g[c]
                if j == 0:
                    ahead = jnp.maximum(vext[0, vx + 1], 0.0) * gext[c, gx + 1]
                    behind = jnp.minimum(vext[0, vx - 1], 0.0) * gext[c, gx - 1]
                    before, after = vext[c, vx - 1], vext[c, vx + 1]
                elif j == 1:
                    ahead = shift_rows(positive[1] * g[c], -1)
                    behind = shift_rows(negative[1] * g[c], 1)
                    before, after = shift_rows(v[c], 1), shift_rows(v[c], -1)
                else:
                    ahead = roll(positive[2] * g[c], -1)
                    behind = roll(negative[2] * g[c], 1)
                    before, after = roll(v[c], 1), roll(v[c], -1)
                totals[c] = totals[c] + here - ahead + behind
                rising, falling = v[c] - before, after - v[c]
                level = 0.5 * (rising + falling)
                slope = slope + g[c] * jnp.where(
                    v[j] > 0.0, rising, jnp.where(v[j] < 0.0, falling, level)
                )
            slopes.append(slope)
        for c in range(3):
            out[c, x] = (g[c] - STEP * totals[c] - STEP * slopes[c])[8:24]

    store = pltpu.make_async_copy(out, out_hbm, load_sem.at[7 + TABLES])
    store.start()
    got7()
    store.wait()
    for wait in pending:
        wait()


def hand_out(grad, sums, out, out_first, out_bias, out_second):
    out[...] = grad[...]
    lane = lanes()
    spare = jnp.where(lane < 41, roll(sums[0:8], -82), roll(sums[8:16], -41))
    both = (sums[0:16], jnp.concatenate([sums[16:24], spare], axis=0))
    for kind, ref in enumerate((out_first, out_second)):
        turned = both[kind].T
        for tap in range(27):
            ref[tap // 9, tap // 3 % 3, tap % 3] = turned[3 * tap : 3 * tap + 3]
        if kind == 0:
            out_bias[...] = turned[81:82]


def local(velocity, cotangents, lead_table, lead_index, first_kernel, first_bias, second_kernel):
    constants = tables()

    def v(*shape, kind=F32):
        return pltpu.VMEM(shape, kind)

    dma = pltpu.SemaphoreType.DMA
    in_vmem = pl.BlockSpec(memory_space=pltpu.VMEM)
    anywhere = pl.BlockSpec(memory_space=pl.ANY)
    shapes = tuple(
        jax.ShapeDtypeStruct(shape, F32)
        for shape in ((3, 2, 16, N), (3, 3, 3, 3, 16), (1, 16), (3, 3, 3, 3, 16))
    )
    results = pl.pallas_call(
        kernel,
        out_shape=(shapes[0], jax.ShapeDtypeStruct((24, N), F32)),
        in_specs=[anywhere] * (7 + TABLES),
        out_specs=(anywhere,) * 2,
        scratch_shapes=[
            v(4, 3, 2, 16, N), pltpu.SMEM((8,), F32), pltpu.SMEM((4,), jnp.int32),
            v(3, 3, 3, 3, 16), v(1, 16), v(3, 3, 3, 3, 16),
            *[v(*t.shape, kind=BF16) for t in constants],
            v(128, N), v(128, N), v(128, N), v(128, N), v(192, N), v(192, N), v(384, N), v(384, N),
            v(24, N), v(24, N), v(3, N), v(192, N), v(3, N), v(3, 2, 16, N),
            v(3, 6, 32, N), v(288, N), v(288, N), v(3, 2, 16, N),
            v(144, 2048, kind=BF16), v(144, 2048, kind=BF16),
            v(144, 2048, kind=BF16), v(144, 2048, kind=BF16),
            v(32, 2048), v(32, 2048, kind=BF16), v(32, 2048, kind=BF16),
            v(144, 2048), v(288, N), v(3, 4, 32, N),
            v(2, 3, 16, N), v(2, 3, 2, 8, N), v(4, 3, 8, N), v(3, 4, 32, N),
            v(N, N), dma((7,)), dma((7,)), dma((7,)), dma((8,)), dma((8,)), dma((8,)), dma((8,)),
            dma((4,)), dma((4,)), dma((8 + TABLES,)), pltpu.SemaphoreType.REGULAR,
        ],
        compiler_params=pltpu.CompilerParams(
            collective_id=0, has_side_effects=True, vmem_limit_bytes=60 * 1024 * 1024
        ),
        name="step_backward",
    )(
        cotangents, velocity, lead_table, lead_index,
        jnp.transpose(first_kernel, (1, 2, 3, 4, 0)), first_bias[None],
        jnp.transpose(second_kernel, (0, 2, 3, 4, 1)), *[jnp.asarray(t) for t in constants],
    )
    grad, first, bias, second = pl.pallas_call(
        hand_out,
        out_shape=shapes,
        in_specs=[in_vmem] * 2,
        out_specs=(in_vmem,) * 4,
        name="hand_out",
    )(*results)
    return (
        grad,
        jnp.transpose(first, (4, 0, 1, 2, 3)),
        bias[0],
        jnp.transpose(second, (0, 4, 1, 2, 3)),
    )


def solution(mesh):
    placed = (
        P(None, "wide", "narrow", None),
        P(None, None, "wide", "narrow", None),
        P(),
        P(),
        P(),
        P(),
        P(),
    )
    return jax.shard_map(
        local,
        mesh=mesh,
        in_specs=placed,
        out_specs=(P(None, "wide", "narrow", None), P(), P(), P()),
        check_vma=False,
    )
```

```python
import math

import jax
import jax.numpy as jnp
import ml_dtypes
import numpy as np
from jax import lax
from jax.experimental import pallas as pl
from jax.experimental.pallas import tpu as pltpu
from jax.sharding import PartitionSpec as P

F32 = jnp.float32
BF16 = jnp.bfloat16
MESH = pl.DeviceIdType.MESH
N = 128
WIDE = 64
NARROW = 8
STEP = 0.25
BIAS = 108
TABLES = 7
ORDER = (2, 0, 1)


def basis(kind, wave):
    cell = np.arange(N)
    if kind == 0 and wave == 0:
        return np.full(N, 1.0 / math.sqrt(N))
    if kind == 1 and wave == 0:
        return (1.0 - 2.0 * (cell % 2)) / math.sqrt(N)
    angle = 2.0 * np.pi * (cell * wave % N) / N
    return math.sqrt(2.0 / N) * (np.cos(angle) if kind == 0 else np.sin(angle))


def halves(table):
    high = table.astype(np.float32).astype(ml_dtypes.bfloat16)
    low = (table - high.astype(np.float64)).astype(np.float32).astype(ml_dtypes.bfloat16)
    return high, low


def left_factor(table):
    high, low = halves(table)
    return np.stack([high, low, high])


def thin_factor(table):
    high, low = halves(table)
    return np.stack([np.concatenate([high, low], axis=1), np.pad(high, ((0, 0), (0, 64)))])


def tables():
    tz = np.stack([basis((i % 16) // 8, 8 * (i // 16) + i % 8) for i in range(N)])
    ty = np.stack([basis(i % 2, i // 2) for i in range(N)])
    tx = np.stack([basis(i // 64, i % 64) for i in range(N)])
    ex = np.concatenate([tx[:, 0::2], tx[:, 1::2]], axis=0)
    txi = np.stack([tx[:, (2 * w - 1 + x) % N] for x in range(4) for w in range(WIDE)])
    cells = []
    for n in range(NARROW):
        cells += [16 * n + r for r in range(16)] + [16 * n - 1, 16 * n + 16] + [0] * 6
    tyi = np.concatenate([ty[k::2, np.array(cells) % N].T for k in range(2)], axis=0)
    spread = np.zeros((2, 2, N, 256))
    gather = np.zeros((2, 2, 144, N))
    for x in range(2):
        for c in range(3):
            for dx in range(3):
                for dy in range(3):
                    for dz in range(3):
                        tap = c * 27 + dx * 9 + dy * 3 + dz
                        flat = 4 * (tap // 3) + tap % 3
                        lane = (dy * 3 + dz) * 16 + 4 * (x + dx) + c
                        back = ((2 - dy) * 3 + 2 - dz) * 16 + 4 * (x + 2 - dx) + c
                        spread[0, x, flat, lane] = 1.0
                        spread[1, x, flat, back] = 1.0
                        gather[0, x, lane, tap] = 1.0
                        gather[1, x, back, tap] = 1.0
        spread[0, x, BIAS, 4 * 16 + 3] = 1.0
        gather[0, x, 4 * 16 + 3, 81] = 1.0
    exact = ml_dtypes.bfloat16
    return (
        left_factor(tz),
        left_factor(ty),
        thin_factor(ex),
        left_factor(txi),
        thin_factor(tyi),
        np.stack([spread[..., :N], spread[..., N:]], axis=2).astype(exact),
        gather.astype(exact),
    )


def split(value):
    high = value.astype(BF16)
    return high, (value - high.astype(F32)).astype(BF16)


def dot(a, b, dims):
    return lax.dot_general(
        a, b, (((dims[0],), (dims[1],)), ((), ())), preferred_element_type=F32
    )


def left(ref):
    return jnp.concatenate([ref[i] for i in range(ref.shape[0])], axis=1)


def right(value, axis=0):
    high, low = split(value)
    return jnp.concatenate([high, high, low], axis=axis)


def stacked(pair, other, dims):
    rows = pair[0].shape[0]
    both = dot(jnp.concatenate(pair, axis=0), other[0], dims)
    return both[:rows] + both[rows:] + dot(pair[0], other[1], dims)


def roll(value, shift):
    return pltpu.roll(value, shift % value.shape[1], 1)


def lanes():
    return lax.broadcasted_iota(jnp.int32, (1, N), 1)


def swap_blocks(m):
    lane = lanes()
    for bit in (1, 2, 4):
        size = 16 * bit
        odd = (lane // size) % 2 == 1
        parts = []
        for i in range(0, N, 2 * size):
            low, high = m[i : i + size], m[i + size : i + 2 * size]
            parts.append(jnp.where(odd, roll(high, size), low))
            parts.append(jnp.where(odd, high, roll(low, -size)))
        m = jnp.concatenate(parts, axis=0)
    return m


def thin(table, value):
    high, low = split(value)
    return dot(table, jnp.concatenate([high, high, low, jnp.zeros_like(low)], axis=0), (1, 0))


def from_pairs(even, odd, first, second):
    lane = lanes()
    one = even[:, first] + roll(odd[:, first], -48)
    two = roll(even[:, second], 48) + odd[:, second]
    return jnp.where(lane < 48, one, jnp.where(lane < 96, two, 0.0))


def project(field, w, n):
    lane = lanes()
    row = lax.broadcasted_iota(jnp.int32, (N, 1), 0)
    block = lane // 16
    comp = block % 3
    is_sin_z = block // 3 % 2 == 1
    slot = lane % 16
    inside = lane < 96
    wave_x = 8 * n + slot % 8
    nyq_x = jnp.logical_and(slot == 8, n == 0)
    nyq_y = row == 64
    nyq_z = jnp.logical_and(is_sin_z, w == 0)
    kx = jnp.where(nyq_x, 64, wave_x).astype(F32)
    ky = jnp.where(nyq_y, 64, row % 64).astype(F32)
    kz = jnp.where(nyq_z, 64, w).astype(F32)
    inverse = 1.0 / jnp.maximum(kx * kx + ky * ky + kz * kz, 1.0)
    dx = jnp.where(slot < 8, wave_x, -wave_x).astype(F32)
    dy = jnp.where(row < 64, row % 64, -(row % 64)).astype(F32)
    dz = jnp.where(is_sin_z, -w, w).astype(F32)
    nyquist = jnp.where(
        comp == 0,
        jnp.where(nyq_x, 64.0, 0.0),
        jnp.where(comp == 2, jnp.where(nyq_z, 64.0, 0.0), 0.0),
    )
    nyquist = nyquist + jnp.where(jnp.logical_and(comp == 1, nyq_y), 64.0, 0.0)

    def derive(v):
        along_x = dx * jnp.where(slot < 8, roll(v, -8), roll(v, 8))
        along_y = dy * jnp.concatenate([v[64:], v[:64]], axis=0)
        along_z = dz * jnp.where(is_sin_z, roll(v, 48), roll(v, -48))
        return jnp.where(comp == 0, along_x, jnp.where(comp == 1, along_y, along_z))

    def over_components(v):
        total = (v + roll(v, -16) + roll(v, -32)) * inverse
        total = jnp.where(jnp.logical_and(inside, comp == 0), total, 0.0)
        return total + roll(total, 16) + roll(total, 32)

    main = over_components(derive(field))
    rest = over_components(nyquist * field)
    return field + derive(main) - nyquist * rest


def z_blocks(received):
    def pick(tile, first, count):
        return [received[48 * n + 24 * tile + first :][:count] for n in range(NARROW)]

    inner = [swap_blocks(jnp.concatenate(pick(tile, 0, 16), axis=0))[:96] for tile in range(2)]
    outer = [piece for pair in zip(pick(0, 16, 8), pick(1, 16, 8)) for piece in pair]
    return jnp.concatenate(inner + [swap_blocks(jnp.concatenate(outer, axis=0))[:96]], axis=0)


def taps(field, high_ref, low_ref):
    for dz in range(3):
        moved = field if dz == 1 else roll(field, 1 - dz)
        for ref, part in zip((high_ref, low_ref), split(moved)):
            for dy in range(3):
                at = (3 * dy + dz) * 16
                for y in range(16):
                    ref[at : at + 16, N * y : N * y + N] = part[16 * (y + dy) : 16 * (y + dy) + 16]


def shift_rows(value, by):
    return pltpu.roll(value, by % value.shape[0], 0)


def kernel(
    cot_hbm, vel_hbm, table_hbm, index_hbm, first_hbm, bias_hbm, second_hbm, *refs
):
    tables_hbm, refs = refs[:TABLES], refs[TABLES:]
    (out_hbm, sums_hbm), refs = refs[:2], refs[2:]
    (cot, table, index, first, bias, second), refs = refs[:6], refs[6:]
    (tz, ty, ex, txi, tyi, spread, gather), refs = refs[:TABLES], refs[TABLES:]
    (
    send1, recv1, send2, recv2, send3, recv3, send4, recv4,
    part, recv5, mine, recv6, whole, out,
    vext, adv, proj, proj_own, adv_hi, adv_lo, proj_hi, proj_lo,
    hidden, hid_hi, hid_lo, scattered, gpart, hext, face_x, face_y, corner, gext,
    flat, own_sem, send_sem, recv_sem, vel_send, vel_recv, e1_send, e1_recv,
    load_sem, token,
    ) = refs
    w = lax.axis_index("wide")
    n = lax.axis_index("narrow")
    wy, wz, wx = w // 16, w // 4 % 4, w % 4
    zl, core = n // 2, n % 2
    ahead_w, behind_w = lax.rem(w + 1, WIDE), lax.rem(w + WIDE - 1, WIDE)
    above, below = lax.rem(n + 1, NARROW), lax.rem(n + NARROW - 1, NARROW)

    far = lax.rem(n + 4, NARROW)
    longer = jnp.where(zl < 2, 1, 3)

    def each_wide(act):
        def offset(i):
            return jnp.where(i < 2, 2 + i, 3 - i)

        for pair in ((2, longer), (0, lax.rem(longer + 2, 4))):
            zs = [lax.rem(wz + oz, 4) * 4 for oz in pair]

            def body(i, carry, zs=zs):
                place = lax.rem(wy + offset(i // 4), 4) * 16 + lax.rem(wx + offset(i % 4), 4)
                for z in zs:
                    act(place + z)
                return carry

            lax.fori_loop(0, 16, body, 0)

    def each_plane(act):
        def body(i, carry):
            act(lax.rem(wy + i // 4, 4) * 16 + wz * 4 + lax.rem(wx + i % 4, 4))
            return carry

        lax.fori_loop(1, 16, body, 0)

    def each_narrow(act):
        for i in (4, 5, 3, 2, 6, 7, 1):
            act(lax.rem(n + i, NARROW))

    member = 2 * wx + core
    height = 4 * wz + zl

    def far_first(i):
        return jnp.where(i < 2, 2 + i, 3 - i)

    def each_member(act):
        for i in (4, 5, 3, 2, 6, 7, 1):
            act(lax.rem(member + i, NARROW))

    def each_height(act):
        def body(i, carry):
            act(lax.rem(height + 8 + jnp.where(i % 2 == 1, (i + 1) // 2, -(i // 2)), 16))
            return carry

        lax.fori_loop(0, 15, body, 0)

    def each_level(act):
        def body(i, carry):
            y, x = lax.rem(wy + far_first(i // 8), 4), lax.rem(wx + far_first(i // 2 % 4), 4)
            act(8 * y + 2 * x + lax.rem(core + 1 - i % 2, 2))
            return carry

        lax.fori_loop(0, 31, body, 0)

    across = (WIDE, each_wide, lambda p: (p, far), None, w)
    narrow = (NARROW, each_narrow, lambda p: (w, p), n, n)
    members = (
        NARROW,
        each_member,
        lambda p: (w - wx + p // 2, n - core + p % 2),
        member,
        member,
    )
    heights = (
        16,
        each_height,
        lambda p: (16 * wy + p // 4 * 4 + wx, p % 4 * 2 + core),
        height,
        height,
    )
    level = (
        32,
        each_level,
        lambda p: (p // 8 * 16 + 4 * wz + p // 2 % 4, n - core + p % 2),
        8 * wy + member,
        8 * wy + member,
    )

    barrier = pltpu.get_barrier_semaphore()

    def greet(device):
        pl.semaphore_signal(barrier, inc=1, device_id=device, device_id_type=MESH)

    for i in (2, 1, 3):
        greet((16 * wy + 4 * lax.rem(wz + i, 4) + wx, far))
    each_plane(lambda p: greet((p, n)))
    neighbours = (
        (ahead_w, n), (behind_w, n), (w, above), (w, below),
        (ahead_w, above), (ahead_w, below), (behind_w, above), (behind_w, below),
    )
    each_narrow(lambda p: greet((w, p)))
    for device in neighbours[:2] + neighbours[4:]:
        greet(device)

    loads = [
        pltpu.make_async_copy(source, target, load_sem.at[i])
        for i, (source, target) in enumerate(
            [
                (cot_hbm, cot),
                (table_hbm, table),
                (index_hbm, index),
                (tables_hbm[0], tz),
                (vel_hbm, vext.at[:, pl.ds(2, 2), pl.ds(8, 16), :]),
                (first_hbm, first),
                (bias_hbm, bias),
                (second_hbm, second),
            ]
            + list(zip(tables_hbm[1:], (ty, ex, txi, tyi, spread, gather)))
        )
    ]
    for load in loads:
        load.start()

    for load in loads[:4]:
        load.wait()
    weight = [table[index[l]] for l in range(4)]
    pieces = []
    for x in range(2):
        for c in ORDER:
            total = weight[0] * cot[0, c, x]
            for l in range(1, 4):
                total = total + weight[l] * cot[l, c, x]
            pieces.append(total)
    pieces.append(jnp.zeros((32, N), F32))
    combined = jnp.concatenate(pieces, axis=0)
    send1[...] = dot(left(tz), right(combined, 1), (1, 1))

    for load in loads[4:]:
        load.wait()

    pl.semaphore_wait(barrier, 3 + 15 + 7 + 6)
    pending = []

    def copies(moves, sends, recvs):
        made = []
        for i, (source, target, device) in enumerate(moves):
            made.append(
                pltpu.make_async_remote_copy(
                    source, target, sends.at[i], recvs.at[i], device_id=device, device_id_type=MESH
                )
            )
        for copy in made:
            copy.start()
            pending.append(copy.wait_send)
        return made

    def exchange(i, group, rows, source, target, used=None):
        size, each, device, own, slot = group

        def block(ref, p):
            return ref.at[pl.ds(p * rows, used or rows)]

        def piece(p):
            return source if source.shape[0] == rows else block(source, p)

        def copy(a, b, to):
            return pltpu.make_async_remote_copy(
                a, b, send_sem.at[i], recv_sem.at[i], device_id=to, device_id_type=MESH
            )

        each(lambda p: copy(piece(p), block(target, slot), device(p)).start())
        some = target if own is None else target.at[pl.ds(0, (size - 1) * (used or rows))]
        others = copy(some, some, (w, far))
        pending.append(others.wait_send)
        if own is None:
            return others.wait_recv
        keep = pltpu.make_async_copy(piece(own), block(target, slot), own_sem.at[i])
        keep.start()

        def arrived():
            keep.wait()
            others.wait_recv()

        return arrived

    got1 = exchange(0, narrow, 16, send1, recv1)

    def tell(p):
        pl.semaphore_signal(token, inc=1, device_id=(p, n), device_id_type=MESH)

    each_plane(tell)

    got1()
    send2[...] = dot(left(ty), right(swap_blocks(recv1[...].T)), (1, 0))
    pl.semaphore_wait(token, 15)
    got2 = exchange(1, across, 2, send2, recv2)

    low, high, full = pl.ds(8, 2), pl.ds(22, 2), pl.ds(8, 16)
    moves = []
    for device, rows, xs, ys in zip(
        neighbours,
        (full, full, high, low, high, low, high, low),
        (0, 4, 2, 2, 0, 0, 4, 4),
        (full, full, pl.ds(6, 2), pl.ds(24, 2)) + (pl.ds(6, 2), pl.ds(24, 2)) * 2,
    ):
        source = vext.at[:, pl.ds(2, 2), rows, :]
        moves.append((source, vext.at[:, pl.ds(xs, 2), ys, :], device))
    vel_copies = copies(moves, vel_send, vel_recv)

    taps_first, taps_second = [], []
    for kind, (ref, place) in enumerate(((first, taps_first), (second, taps_second))):
        flat[...] = jnp.zeros_like(flat)
        for tap in range(27):
            flat[4 * tap : 4 * tap + 3, 0:16] = ref[tap // 9, tap // 3 % 3, tap % 3]
        if kind == 0:
            flat[BIAS : BIAS + 1, 0:16] = bias[...]
        for piece in split(flat[...]):
            rows = []
            for x in range(2):
                cols = [dot(piece, spread[kind, x, i], (0, 0))[:16] for i in range(2)]
                rows.append(jnp.concatenate(cols, axis=1)[:, :144])
            place.append(jnp.concatenate(rows, axis=0).astype(BF16))

    proj[...] = jnp.zeros_like(proj)
    face_y[...] = jnp.zeros_like(face_y)
    corner[...] = jnp.zeros_like(corner)
    gext[...] = jnp.zeros_like(gext)
    vext[:, :, 0:6] = jnp.zeros((3, 6, 6, N), F32)
    vext[:, :, 26:32] = jnp.zeros((3, 6, 6, N), F32)
    sublane = lax.broadcasted_iota(jnp.int32, (288, N), 0) % 16
    adv[...] = jnp.where(sublane == 3, 1.0, 0.0)

    got2()
    pair = jnp.concatenate([recv2[pl.ds(k, 64, stride=2), :] for k in range(2)], axis=1)
    field = thin(left(ex), pair)
    first_half, second_half = slice(0, N), slice(N, 2 * N)
    spectrum = project(from_pairs(field[:N], field[N:], first_half, second_half), w, far)
    fields = dot(left(txi), right(spectrum), (1, 0))
    lane = lanes()
    last = fields[192:256]
    for x in range(3):
        rows = jnp.where(lane < 96, fields[64 * x : 64 * x + 64], roll(last, 96 - 32 * x))
        send3[pl.ds(x, 64, stride=3), :] = rows
    got3 = exchange(2, across, 3, send3, recv3)

    for copy in vel_copies:
        copy.wait_recv()
    for x in range(4):
        v = [vext[c, x + 1] for c in range(3)]
        totals = [jnp.zeros((32, N), F32)] * 3
        for j in range(3):
            positive, negative = jnp.maximum(v[j], 0.0), jnp.minimum(v[j], 0.0)
            for c in range(3):
                if j == 0:
                    before, after = vext[c, x], vext[c, x + 2]
                elif j == 1:
                    before, after = shift_rows(v[c], 1), shift_rows(v[c], -1)
                else:
                    before, after = roll(v[c], 1), roll(v[c], -1)
                totals[c] = totals[c] + positive * (v[c] - before) + negative * (after - v[c])
        for c in range(3):
            done = v[c] - STEP * totals[c]
            at = 4 * x + c
            adv[at : at + 1] = done[7:8]
            adv[pl.ds(16 + at, 16, stride=16), :] = done[8:24]
            adv[272 + at : 273 + at] = done[24:25]
    taps(adv[...], adv_hi, adv_lo)
    adv_taps = (adv_hi[...], adv_lo[...])
    hid = jnp.tanh(stacked(taps_first, adv_taps, (1, 0)))
    hidden[...] = 1.0 - hid * hid
    hid_hi[...], hid_lo[...] = split(hid)

    got3()
    rows = [recv3[pl.ds(x, 64, stride=3), :] for x in range(3)]
    rows.append(
        jnp.where(lane < 32, roll(rows[0], 32), jnp.where(lane < 64, roll(rows[1], 64), roll(rows[2], 96)))
    )
    field = thin(left(tyi), jnp.concatenate(rows, axis=1))
    for tile in range(2):
        columns_of = [slice(N * x, N * x + N) for x in (2 * tile, 2 * tile + 1)]
        pieces = from_pairs(field[:192], field[192:], *columns_of)
        for i in range(NARROW):
            send4[48 * i + 24 * tile : 48 * i + 24 * tile + 24] = pieces[24 * i : 24 * i + 24]
    got4 = exchange(3, narrow, 48, send4, recv4, 42)

    got4()
    spectra = right(z_blocks(recv4[...]), 1)
    fields = dot(spectra, jnp.concatenate([tz[i] for i in range(3)], axis=0), (1, 0))
    for x in range(4):
        for place, c in enumerate(ORDER):
            block = 3 * x + place
            inner = fields[16 * block : 16 * block + 16]
            outer = fields[192 + 16 * (block % 6) + 8 * (x // 2) :][:8]
            at = 4 * x + c
            proj[at : at + 1] = outer[0:1]
            proj[pl.ds(16 + at, 16, stride=16), :] = inner
            proj[272 + at : 273 + at] = outer[1:2]
            if x in (1, 2):
                proj_own[c, x - 1] = inner

    taps(proj[...], proj_hi, proj_lo)
    proj_taps = (proj_hi[...], proj_lo[...])
    pre = split(stacked(taps_second, proj_taps, (1, 0)) * hidden[...])

    gradients = []
    for kind, (rows, cols) in enumerate(((pre, adv_taps), ((hid_hi[...], hid_lo[...]), proj_taps))):
        raw = stacked(rows, cols, (1, 1))
        total = jnp.zeros((16, N), F32)
        for x in range(2):
            pair = jnp.concatenate(split(raw[16 * x : 16 * x + 16]), axis=0)
            pair = dot(pair, gather[kind, x], (1, 0))
            total = total + pair[:16] + pair[16:]
        gradients.append(total)
    lane = lanes()
    beside = jnp.logical_and(lane >= 82, lane < 123)
    spare = gradients[1][8:]
    part[0:8] = jnp.where(beside, roll(spare, 82), gradients[0][:8])
    part[8:16] = jnp.where(beside, roll(spare, 41), gradients[0][8:])
    part[16:24] = gradients[1][:8]
    got5 = exchange(4, members, 3, part, recv5)

    scattered[...] = dot(
        jnp.concatenate([*taps_first, taps_first[0]], axis=0),
        jnp.concatenate([pre[0], pre[0], pre[1]], axis=0),
        (0, 0),
    )
    for y in range(18):
        moved = []
        for dz in range(3):
            total = None
            for dy in range(3):
                if 0 <= y - dy < 16:
                    at = (3 * dy + dz) * 16
                    term = scattered[at : at + 16, N * (y - dy) : N * (y - dy) + N]
                    total = term if total is None else total + term
            moved.append(total if dz == 1 else roll(total, dz - 1))
        gpart[16 * y : 16 * y + 16] = moved[0] + moved[1] + moved[2]
    for x in range(4):
        for c in range(3):
            at = 4 * x + c
            gext[c, x + 1, 7:8] = gpart[at : at + 1]
            middle = gpart[pl.ds(16 + at, 16, stride=16), :]
            gext[c, x + 1, 8:24] = middle + proj_own[c, x - 1] if x in (1, 2) else middle
            gext[c, x + 1, 24:25] = gpart[272 + at : 273 + at]

    for c in range(3):
        hext[c, 0] = STEP * (jnp.maximum(vext[0, 1], 0.0) * gext[c, 1])
        hext[c, 5] = -STEP * (jnp.minimum(vext[0, 4], 0.0) * gext[c, 4])
    for x in range(1, 5):
        v = [vext[c, x] for c in range(3)]
        g = [gext[c, x] for c in range(3)]
        positive = [jnp.maximum(a, 0.0) for a in v]
        negative = [jnp.minimum(a, 0.0) for a in v]
        totals = [jnp.zeros((32, N), F32)] * 3
        slopes = []
        for j in range(3):
            slope = jnp.zeros((32, N), F32)
            for c in range(3):
                here = (positive[j] - negative[j]) * g[c]
                if j == 0:
                    ahead = jnp.maximum(vext[0, x + 1], 0.0) * gext[c, x + 1]
                    behind = jnp.minimum(vext[0, x - 1], 0.0) * gext[c, x - 1]
                    before, after = vext[c, x - 1], vext[c, x + 1]
                elif j == 1:
                    ahead = shift_rows(positive[1] * g[c], -1)
                    behind = shift_rows(negative[1] * g[c], 1)
                    before, after = shift_rows(v[c], 1), shift_rows(v[c], -1)
                else:
                    ahead = roll(positive[2] * g[c], -1)
                    behind = roll(negative[2] * g[c], 1)
                    before, after = roll(v[c], 1), roll(v[c], -1)
                totals[c] = totals[c] + here - ahead + behind
                rising, falling = v[c] - before, after - v[c]
                level_slope = 0.5 * (rising + falling)
                slope = slope + g[c] * jnp.where(
                    v[j] > 0.0, rising, jnp.where(v[j] < 0.0, falling, level_slope)
                )
            slopes.append(slope)
        for c in range(3):
            hext[c, x] = g[c] - STEP * totals[c] - STEP * slopes[c]

    got5()

    def fold(ref):
        count = ref.shape[0] // 3
        return [
            jnp.sum(ref[pl.ds(row, count, stride=3), :], axis=0, keepdims=True) for row in range(3)
        ]

    for row, total in enumerate(fold(recv5)):
        mine[row : row + 1] = total
    got6 = exchange(5, heights, 3, mine, recv6)

    before_x, own_x, after_x = pl.ds(0, 2), pl.ds(2, 2), pl.ds(4, 2)
    before_y, own_y, after_y = pl.ds(6, 2), pl.ds(8, 16), pl.ds(24, 2)
    first_y, last_y = pl.ds(0, 2), pl.ds(6, 2)
    shared = copies(
        [
            (hext.at[:, after_x, own_y, :], face_x.at[0], (ahead_w, n)),
            (hext.at[:, before_x, own_y, :], face_x.at[1], (behind_w, n)),
            (hext.at[:, own_x, after_y, :], face_y.at[0, :, :, first_y, :], (w, above)),
            (hext.at[:, own_x, before_y, :], face_y.at[1, :, :, last_y, :], (w, below)),
            (hext.at[:, after_x, after_y, :], corner.at[0, :, :, first_y, :], (ahead_w, above)),
            (hext.at[:, after_x, before_y, :], corner.at[1, :, :, last_y, :], (ahead_w, below)),
            (hext.at[:, before_x, after_y, :], corner.at[2, :, :, first_y, :], (behind_w, above)),
            (hext.at[:, before_x, before_y, :], corner.at[3, :, :, last_y, :], (behind_w, below)),
        ],
        e1_send,
        e1_recv,
    )

    got6()
    for row, total in enumerate(fold(recv6)):
        whole[row : row + 1] = total * (N * N * N) ** -0.5
    got7 = exchange(6, level, 3, whole, sums_hbm)

    for copy in shared:
        copy.wait_recv()
    for c in range(3):
        for x in range(2):
            own = hext[c, x + 2, 8:24] + face_x[0, c, x] + face_x[1, c, x]
            out[c, x, 0:8] = own[0:8] + face_y[0, c, x] + corner[0, c, x] + corner[2, c, x]
            out[c, x, 8:16] = own[8:16] + face_y[1, c, x] + corner[1, c, x] + corner[3, c, x]
    store = pltpu.make_async_copy(out, out_hbm, load_sem.at[7 + TABLES])
    store.start()
    for wait in pending[:-1]:
        wait()
    store.wait()
    got7()
    pending[-1]()


def hand_out(grad, sums, out, out_first, out_bias, out_second):
    out[...] = grad[...]
    lane = lanes()
    total = sums[0:24] + sums[24:48] + sums[48:72] + sums[72:96]
    spare = jnp.where(lane < 41, roll(total[0:8], -82), roll(total[8:16], -41))
    both = (total[0:16], jnp.concatenate([total[16:24], spare], axis=0))
    for kind, ref in enumerate((out_first, out_second)):
        turned = both[kind].T
        for tap in range(27):
            ref[tap // 9, tap // 3 % 3, tap % 3] = turned[3 * tap : 3 * tap + 3]
        if kind == 0:
            out_bias[...] = turned[81:82]


def local(velocity, cotangents, lead_table, lead_index, first_kernel, first_bias, second_kernel):
    constants = tables()

    def v(*shape, kind=F32):
        return pltpu.VMEM(shape, kind)

    dma = pltpu.SemaphoreType.DMA
    in_vmem = pl.BlockSpec(memory_space=pltpu.VMEM)
    anywhere = pl.BlockSpec(memory_space=pl.ANY)
    shapes = tuple(
        jax.ShapeDtypeStruct(shape, F32)
        for shape in ((3, 2, 16, N), (3, 3, 3, 3, 16), (1, 16), (3, 3, 3, 3, 16))
    )
    results = pl.pallas_call(
        kernel,
        out_shape=(shapes[0], jax.ShapeDtypeStruct((96, N), F32)),
        in_specs=[anywhere] * (7 + TABLES),
        out_specs=(anywhere,) * 2,
        scratch_shapes=[
            v(4, 3, 2, 16, N), pltpu.SMEM((8,), F32), pltpu.SMEM((4,), jnp.int32),
            v(3, 3, 3, 3, 16), v(1, 16), v(3, 3, 3, 3, 16),
            *[v(*t.shape, kind=BF16) for t in constants],
            v(128, N), v(128, N), v(128, N), v(128, N), v(192, N), v(192, N), v(384, N), v(384, N),
            v(24, N), v(24, N), v(3, N), v(48, N), v(3, N), v(3, 2, 16, N),
            v(3, 6, 32, N), v(288, N), v(288, N), v(3, 2, 16, N),
            v(144, 2048, kind=BF16), v(144, 2048, kind=BF16),
            v(144, 2048, kind=BF16), v(144, 2048, kind=BF16),
            v(32, 2048), v(32, 2048, kind=BF16), v(32, 2048, kind=BF16),
            v(144, 2048), v(288, N), v(3, 6, 32, N),
            v(2, 3, 2, 16, N), v(2, 3, 2, 8, N), v(4, 3, 2, 8, N), v(3, 6, 32, N),
            v(N, N), dma((7,)), dma((7,)), dma((7,)), dma((8,)), dma((8,)), dma((8,)), dma((8,)),
            dma((8 + TABLES,)), pltpu.SemaphoreType.REGULAR,
        ],
        compiler_params=pltpu.CompilerParams(
            collective_id=0, has_side_effects=True, vmem_limit_bytes=60 * 1024 * 1024
        ),
        name="step_backward",
    )(
        cotangents, velocity, lead_table, lead_index,
        jnp.transpose(first_kernel, (1, 2, 3, 4, 0)), first_bias[None],
        jnp.transpose(second_kernel, (0, 2, 3, 4, 1)), *[jnp.asarray(t) for t in constants],
    )
    grad, first, bias, second = pl.pallas_call(
        hand_out,
        out_shape=shapes,
        in_specs=[in_vmem] * 2,
        out_specs=(in_vmem,) * 4,
        name="hand_out",
    )(*results)
    return (
        grad,
        jnp.transpose(first, (4, 0, 1, 2, 3)),
        bias[0],
        jnp.transpose(second, (0, 4, 1, 2, 3)),
    )


def solution(mesh):
    placed = (
        P(None, "wide", "narrow", None),
        P(None, None, "wide", "narrow", None),
        P(),
        P(),
        P(),
        P(),
        P(),
    )
    return jax.shard_map(
        local,
        mesh=mesh,
        in_specs=placed,
        out_specs=(P(None, "wide", "narrow", None), P(), P(), P()),
        check_vma=False,
    )
```

```python
import math

import jax
import jax.numpy as jnp
import ml_dtypes
import numpy as np
from jax import lax
from jax.experimental import pallas as pl
from jax.experimental.pallas import tpu as pltpu
from jax.sharding import PartitionSpec as P

F32 = jnp.float32
BF16 = jnp.bfloat16
MESH = pl.DeviceIdType.MESH
N = 128
WIDE = 64
NARROW = 8
STEP = 0.25
BIAS = 108
TABLES = 7
ORDER = (2, 0, 1)


def basis(kind, wave):
    cell = np.arange(N)
    if kind == 0 and wave == 0:
        return np.full(N, 1.0 / math.sqrt(N))
    if kind == 1 and wave == 0:
        return (1.0 - 2.0 * (cell % 2)) / math.sqrt(N)
    angle = 2.0 * np.pi * (cell * wave % N) / N
    return math.sqrt(2.0 / N) * (np.cos(angle) if kind == 0 else np.sin(angle))


def halves(table):
    high = table.astype(np.float32).astype(ml_dtypes.bfloat16)
    low = (table - high.astype(np.float64)).astype(np.float32).astype(ml_dtypes.bfloat16)
    return high, low


def left_factor(table):
    high, low = halves(table)
    return np.stack([high, low, high])


def thin_factor(table):
    high, low = halves(table)
    return np.stack([np.concatenate([high, low], axis=1), np.pad(high, ((0, 0), (0, 64)))])


def tables():
    tz = np.stack([basis((i % 16) // 8, 8 * (i // 16) + i % 8) for i in range(N)])
    ty = np.stack([basis(i % 2, i // 2) for i in range(N)])
    tx = np.stack([basis(i // 64, i % 64) for i in range(N)])
    ex = np.concatenate([tx[:, 0::2], tx[:, 1::2]], axis=0)
    txi = np.stack([tx[:, (2 * w - 1 + x) % N] for x in range(4) for w in range(WIDE)])
    cells = []
    for n in range(NARROW):
        cells += [16 * n + r for r in range(16)] + [16 * n - 1, 16 * n + 16] + [0] * 6
    tyi = np.concatenate([ty[k::2, np.array(cells) % N].T for k in range(2)], axis=0)
    spread = np.zeros((2, 2, N, 256))
    gather = np.zeros((2, 2, 144, N))
    for x in range(2):
        for c in range(3):
            for dx in range(3):
                for dy in range(3):
                    for dz in range(3):
                        tap = c * 27 + dx * 9 + dy * 3 + dz
                        flat = 4 * (tap // 3) + tap % 3
                        lane = (dy * 3 + dz) * 16 + 4 * (x + dx) + c
                        back = ((2 - dy) * 3 + 2 - dz) * 16 + 4 * (x + 2 - dx) + c
                        spread[0, x, flat, lane] = 1.0
                        spread[1, x, flat, back] = 1.0
                        gather[0, x, lane, tap] = 1.0
                        gather[1, x, back, tap] = 1.0
        spread[0, x, BIAS, 4 * 16 + 3] = 1.0
        gather[0, x, 4 * 16 + 3, 81] = 1.0
    exact = ml_dtypes.bfloat16
    return (
        left_factor(tz),
        left_factor(ty),
        thin_factor(ex),
        left_factor(txi),
        thin_factor(tyi),
        np.stack([spread[..., :N], spread[..., N:]], axis=2).astype(exact),
        gather.astype(exact),
    )


def split(value):
    high = value.astype(BF16)
    return high, (value - high.astype(F32)).astype(BF16)


def dot(a, b, dims):
    return lax.dot_general(
        a, b, (((dims[0],), (dims[1],)), ((), ())), preferred_element_type=F32
    )


def left(ref):
    return jnp.concatenate([ref[i] for i in range(ref.shape[0])], axis=1)


def right(value, axis=0):
    high, low = split(value)
    return jnp.concatenate([high, high, low], axis=axis)


def stacked(pair, other, dims):
    rows = pair[0].shape[0]
    both = dot(jnp.concatenate(pair, axis=0), other[0], dims)
    return both[:rows] + both[rows:] + dot(pair[0], other[1], dims)


def roll(value, shift):
    return pltpu.roll(value, shift % value.shape[1], 1)


def lanes():
    return lax.broadcasted_iota(jnp.int32, (1, N), 1)


def swap_blocks(m):
    lane = lanes()
    for bit in (1, 2, 4):
        size = 16 * bit
        odd = (lane // size) % 2 == 1
        parts = []
        for i in range(0, N, 2 * size):
            low, high = m[i : i + size], m[i + size : i + 2 * size]
            parts.append(jnp.where(odd, roll(high, size), low))
            parts.append(jnp.where(odd, high, roll(low, -size)))
        m = jnp.concatenate(parts, axis=0)
    return m


def thin(table, value):
    high, low = split(value)
    return dot(table, jnp.concatenate([high, high, low, jnp.zeros_like(low)], axis=0), (1, 0))


def from_pairs(even, odd, first, second):
    lane = lanes()
    one = even[:, first] + roll(odd[:, first], -48)
    two = roll(even[:, second], 48) + odd[:, second]
    return jnp.where(lane < 48, one, jnp.where(lane < 96, two, 0.0))


def project(field, w, n):
    lane = lanes()
    row = lax.broadcasted_iota(jnp.int32, (N, 1), 0)
    block = lane // 16
    comp = block % 3
    is_sin_z = block // 3 % 2 == 1
    slot = lane % 16
    inside = lane < 96
    wave_x = 8 * n + slot % 8
    nyq_x = jnp.logical_and(slot == 8, n == 0)
    nyq_y = row == 64
    nyq_z = jnp.logical_and(is_sin_z, w == 0)
    kx = jnp.where(nyq_x, 64, wave_x).astype(F32)
    ky = jnp.where(nyq_y, 64, row % 64).astype(F32)
    kz = jnp.where(nyq_z, 64, w).astype(F32)
    inverse = 1.0 / jnp.maximum(kx * kx + ky * ky + kz * kz, 1.0)
    dx = jnp.where(slot < 8, wave_x, -wave_x).astype(F32)
    dy = jnp.where(row < 64, row % 64, -(row % 64)).astype(F32)
    dz = jnp.where(is_sin_z, -w, w).astype(F32)
    nyquist = jnp.where(
        comp == 0,
        jnp.where(nyq_x, 64.0, 0.0),
        jnp.where(comp == 2, jnp.where(nyq_z, 64.0, 0.0), 0.0),
    )
    nyquist = nyquist + jnp.where(jnp.logical_and(comp == 1, nyq_y), 64.0, 0.0)

    def derive(v):
        along_x = dx * jnp.where(slot < 8, roll(v, -8), roll(v, 8))
        along_y = dy * jnp.concatenate([v[64:], v[:64]], axis=0)
        along_z = dz * jnp.where(is_sin_z, roll(v, 48), roll(v, -48))
        return jnp.where(comp == 0, along_x, jnp.where(comp == 1, along_y, along_z))

    def over_components(v):
        total = (v + roll(v, -16) + roll(v, -32)) * inverse
        total = jnp.where(jnp.logical_and(inside, comp == 0), total, 0.0)
        return total + roll(total, 16) + roll(total, 32)

    main = over_components(derive(field))
    rest = over_components(nyquist * field)
    return field + derive(main) - nyquist * rest


def z_blocks(received):
    def pick(tile, first, count):
        return [received[48 * n + 24 * tile + first :][:count] for n in range(NARROW)]

    inner = [swap_blocks(jnp.concatenate(pick(tile, 0, 16), axis=0))[:96] for tile in range(2)]
    outer = [piece for pair in zip(pick(0, 16, 8), pick(1, 16, 8)) for piece in pair]
    return jnp.concatenate(inner + [swap_blocks(jnp.concatenate(outer, axis=0))[:96]], axis=0)


def taps(field, high_ref, low_ref):
    for dz in range(3):
        moved = field if dz == 1 else roll(field, 1 - dz)
        for ref, part in zip((high_ref, low_ref), split(moved)):
            for dy in range(3):
                at = (3 * dy + dz) * 16
                for y in range(16):
                    ref[at : at + 16, N * y : N * y + N] = part[16 * (y + dy) : 16 * (y + dy) + 16]


def shift_rows(value, by):
    return pltpu.roll(value, by % value.shape[0], 0)


def kernel(
    cot_hbm, vel_hbm, table_hbm, index_hbm, first_hbm, bias_hbm, second_hbm, *refs
):
    tables_hbm, refs = refs[:TABLES], refs[TABLES:]
    (out_hbm, sums_hbm), refs = refs[:2], refs[2:]
    (cot, table, index, first, bias, second), refs = refs[:6], refs[6:]
    (tz, ty, ex, txi, tyi, spread, gather), refs = refs[:TABLES], refs[TABLES:]
    (
    send1, recv1, send2, recv2, send3, recv3, send4, recv4,
    part, recv5, mine, recv6, whole, out,
    vext, adv, proj, proj_own, adv_hi, adv_lo, proj_hi, proj_lo,
    hidden, hid_hi, hid_lo, scattered, gpart, hext, face_x, face_y, corner, gext,
    flat, own_sem, send_sem, recv_sem, vel_send, vel_recv, e1_send, e1_recv,
    load_sem, token,
    ) = refs
    w = lax.axis_index("wide")
    n = lax.axis_index("narrow")
    wy, wz, wx = w // 16, w // 4 % 4, w % 4
    zl, core = n // 2, n % 2
    ahead_w, behind_w = lax.rem(w + 1, WIDE), lax.rem(w + WIDE - 1, WIDE)
    above, below = lax.rem(n + 1, NARROW), lax.rem(n + NARROW - 1, NARROW)

    far = lax.rem(n + 4, NARROW)
    longer = jnp.where(zl < 2, 1, 3)

    def each_wide(act):
        ys = [lax.rem(wy + i, 4) * 16 for i in (2, 3, 1, 0)]
        xs = [lax.rem(wx + i, 4) for i in (2, 3, 1, 0)]
        for pair in ((2, longer), (0, lax.rem(longer + 2, 4))):
            zs = [lax.rem(wz + oz, 4) * 4 for oz in pair]

            for y in ys:
                for x in xs:
                    for z in zs:
                        act(y + x + z)

    def each_plane(act):
        def body(i, carry):
            y, x = lax.rem(wy + far_first(i // 4), 4), lax.rem(wx + far_first(i % 4), 4)
            act(y * 16 + wz * 4 + x)
            return carry

        lax.fori_loop(0, 15, body, 0)

    def each_narrow(act):
        for i in (4, 5, 3, 2, 6, 7, 1):
            act(lax.rem(n + i, NARROW))

    member = 2 * wx + core
    height = 4 * wz + zl

    def far_first(i):
        return jnp.where(i < 2, 2 + i, 3 - i)

    def each_member(act):
        for i in (4, 5, 3, 2, 6, 7, 1):
            act(lax.rem(member + i, NARROW))

    def each_height(act):
        def body(i, carry):
            act(lax.rem(height + 8 + jnp.where(i % 2 == 1, (i + 1) // 2, -(i // 2)), 16))
            return carry

        lax.fori_loop(0, 15, body, 0)

    def each_level(act):
        def body(i, carry):
            y, x = lax.rem(wy + far_first(i // 8), 4), lax.rem(wx + far_first(i // 2 % 4), 4)
            act(8 * y + 2 * x + lax.rem(core + 1 - i % 2, 2))
            return carry

        lax.fori_loop(0, 31, body, 0)

    across = (WIDE, each_wide, lambda p: (p, far), None, w)
    narrow = (NARROW, each_narrow, lambda p: (w, p), n, n)
    members = (
        NARROW,
        each_member,
        lambda p: (w - wx + p // 2, n - core + p % 2),
        member,
        member,
    )
    heights = (
        16,
        each_height,
        lambda p: (16 * wy + p // 4 * 4 + wx, p % 4 * 2 + core),
        height,
        height,
    )
    level = (
        32,
        each_level,
        lambda p: (p // 8 * 16 + 4 * wz + p // 2 % 4, n - core + p % 2),
        8 * wy + member,
        8 * wy + member,
    )

    barrier = pltpu.get_barrier_semaphore()

    def greet(device):
        pl.semaphore_signal(barrier, inc=1, device_id=device, device_id_type=MESH)

    for i in (2, 1, 3):
        greet((16 * wy + 4 * lax.rem(wz + i, 4) + wx, far))
    each_plane(lambda p: greet((p, n)))
    neighbours = (
        (ahead_w, n), (behind_w, n), (w, above), (w, below),
        (ahead_w, above), (ahead_w, below), (behind_w, above), (behind_w, below),
    )
    each_narrow(lambda p: greet((w, p)))
    for device in neighbours[:2] + neighbours[4:]:
        greet(device)

    loads = [
        pltpu.make_async_copy(source, target, load_sem.at[i])
        for i, (source, target) in enumerate(
            [
                (cot_hbm, cot),
                (table_hbm, table),
                (index_hbm, index),
                (tables_hbm[0], tz),
                (vel_hbm, vext.at[:, pl.ds(2, 2), pl.ds(8, 16), :]),
                (first_hbm, first),
                (bias_hbm, bias),
                (second_hbm, second),
            ]
            + list(zip(tables_hbm[1:], (ty, ex, txi, tyi, spread, gather)))
        )
    ]
    for load in loads:
        load.start()

    for load in loads[:4]:
        load.wait()
    weight = [table[index[l]] for l in range(4)]
    pieces = []
    for x in range(2):
        for c in ORDER:
            total = weight[0] * cot[0, c, x]
            for l in range(1, 4):
                total = total + weight[l] * cot[l, c, x]
            pieces.append(total)
    pieces.append(jnp.zeros((32, N), F32))
    combined = jnp.concatenate(pieces, axis=0)
    send1[...] = dot(left(tz), right(combined, 1), (1, 1))

    for load in loads[4:]:
        load.wait()

    pl.semaphore_wait(barrier, 3 + 15 + 7 + 6)
    pending = []

    def copies(moves, sends, recvs):
        made = []
        for i, (source, target, device) in enumerate(moves):
            made.append(
                pltpu.make_async_remote_copy(
                    source, target, sends.at[i], recvs.at[i], device_id=device, device_id_type=MESH
                )
            )
        for copy in made:
            copy.start()
            pending.append(copy.wait_send)
        return made

    def exchange(i, group, rows, source, target, used=None):
        size, each, device, own, slot = group

        def block(ref, p):
            return ref.at[pl.ds(p * rows, used or rows)]

        def piece(p):
            return source if source.shape[0] == rows else block(source, p)

        def copy(a, b, to):
            return pltpu.make_async_remote_copy(
                a, b, send_sem.at[i], recv_sem.at[i], device_id=to, device_id_type=MESH
            )

        each(lambda p: copy(piece(p), block(target, slot), device(p)).start())
        some = target if own is None else target.at[pl.ds(0, (size - 1) * (used or rows))]
        others = copy(some, some, (w, far))
        pending.append(others.wait_send)
        if own is None:
            return others.wait_recv
        keep = pltpu.make_async_copy(piece(own), block(target, slot), own_sem.at[i])
        keep.start()

        def arrived():
            keep.wait()
            others.wait_recv()

        return arrived

    got1 = exchange(0, narrow, 16, send1, recv1)

    def tell(p):
        pl.semaphore_signal(token, inc=1, device_id=(p, n), device_id_type=MESH)

    each_plane(tell)

    got1()
    send2[...] = dot(left(ty), right(swap_blocks(recv1[...].T)), (1, 0))
    pl.semaphore_wait(token, 15)
    got2 = exchange(1, across, 2, send2, recv2)

    low, high, full = pl.ds(8, 2), pl.ds(22, 2), pl.ds(8, 16)
    moves = []
    for device, rows, xs, ys in zip(
        neighbours,
        (full, full, high, low, high, low, high, low),
        (0, 4, 2, 2, 0, 0, 4, 4),
        (full, full, pl.ds(6, 2), pl.ds(24, 2)) + (pl.ds(6, 2), pl.ds(24, 2)) * 2,
    ):
        source = vext.at[:, pl.ds(2, 2), rows, :]
        moves.append((source, vext.at[:, pl.ds(xs, 2), ys, :], device))
    vel_copies = copies(moves, vel_send, vel_recv)

    taps_first, taps_second = [], []
    for kind, (ref, place) in enumerate(((first, taps_first), (second, taps_second))):
        flat[...] = jnp.zeros_like(flat)
        for tap in range(27):
            flat[4 * tap : 4 * tap + 3, 0:16] = ref[tap // 9, tap // 3 % 3, tap % 3]
        if kind == 0:
            flat[BIAS : BIAS + 1, 0:16] = bias[...]
        for piece in split(flat[...]):
            rows = []
            for x in range(2):
                cols = [dot(piece, spread[kind, x, i], (0, 0))[:16] for i in range(2)]
                rows.append(jnp.concatenate(cols, axis=1)[:, :144])
            place.append(jnp.concatenate(rows, axis=0).astype(BF16))

    proj[...] = jnp.zeros_like(proj)
    face_y[...] = jnp.zeros_like(face_y)
    corner[...] = jnp.zeros_like(corner)
    gext[...] = jnp.zeros_like(gext)
    vext[:, :, 0:6] = jnp.zeros((3, 6, 6, N), F32)
    vext[:, :, 26:32] = jnp.zeros((3, 6, 6, N), F32)
    sublane = lax.broadcasted_iota(jnp.int32, (288, N), 0) % 16
    adv[...] = jnp.where(sublane == 3, 1.0, 0.0)

    got2()
    pair = jnp.concatenate([recv2[pl.ds(k, 64, stride=2), :] for k in range(2)], axis=1)
    field = thin(left(ex), pair)
    first_half, second_half = slice(0, N), slice(N, 2 * N)
    spectrum = project(from_pairs(field[:N], field[N:], first_half, second_half), w, far)
    fields = dot(left(txi), right(spectrum), (1, 0))
    lane = lanes()
    last = fields[192:256]
    for x in range(3):
        rows = jnp.where(lane < 96, fields[64 * x : 64 * x + 64], roll(last, 96 - 32 * x))
        send3[pl.ds(x, 64, stride=3), :] = rows
    got3 = exchange(2, across, 3, send3, recv3)

    for copy in vel_copies:
        copy.wait_recv()
    for x in range(4):
        v = [vext[c, x + 1] for c in range(3)]
        totals = [jnp.zeros((32, N), F32)] * 3
        for j in range(3):
            positive, negative = jnp.maximum(v[j], 0.0), jnp.minimum(v[j], 0.0)
            for c in range(3):
                if j == 0:
                    before, after = vext[c, x], vext[c, x + 2]
                elif j == 1:
                    before, after = shift_rows(v[c], 1), shift_rows(v[c], -1)
                else:
                    before, after = roll(v[c], 1), roll(v[c], -1)
                totals[c] = totals[c] + positive * (v[c] - before) + negative * (after - v[c])
        for c in range(3):
            done = v[c] - STEP * totals[c]
            at = 4 * x + c
            adv[at : at + 1] = done[7:8]
            adv[pl.ds(16 + at, 16, stride=16), :] = done[8:24]
            adv[272 + at : 273 + at] = done[24:25]
    taps(adv[...], adv_hi, adv_lo)
    adv_taps = (adv_hi[...], adv_lo[...])
    hid = jnp.tanh(stacked(taps_first, adv_taps, (1, 0)))
    hidden[...] = 1.0 - hid * hid
    hid_hi[...], hid_lo[...] = split(hid)

    got3()
    rows = [recv3[pl.ds(x, 64, stride=3), :] for x in range(3)]
    rows.append(
        jnp.where(lane < 32, roll(rows[0], 32), jnp.where(lane < 64, roll(rows[1], 64), roll(rows[2], 96)))
    )
    field = thin(left(tyi), jnp.concatenate(rows, axis=1))
    for tile in range(2):
        columns_of = [slice(N * x, N * x + N) for x in (2 * tile, 2 * tile + 1)]
        pieces = from_pairs(field[:192], field[192:], *columns_of)
        for i in range(NARROW):
            send4[48 * i + 24 * tile : 48 * i + 24 * tile + 24] = pieces[24 * i : 24 * i + 24]
    got4 = exchange(3, narrow, 48, send4, recv4, 42)

    got4()
    spectra = right(z_blocks(recv4[...]), 1)
    fields = dot(spectra, jnp.concatenate([tz[i] for i in range(3)], axis=0), (1, 0))
    for x in range(4):
        for place, c in enumerate(ORDER):
            block = 3 * x + place
            inner = fields[16 * block : 16 * block + 16]
            outer = fields[192 + 16 * (block % 6) + 8 * (x // 2) :][:8]
            at = 4 * x + c
            proj[at : at + 1] = outer[0:1]
            proj[pl.ds(16 + at, 16, stride=16), :] = inner
            proj[272 + at : 273 + at] = outer[1:2]
            if x in (1, 2):
                proj_own[c, x - 1] = inner

    taps(proj[...], proj_hi, proj_lo)
    proj_taps = (proj_hi[...], proj_lo[...])
    pre = split(stacked(taps_second, proj_taps, (1, 0)) * hidden[...])

    gradients = []
    for kind, (rows, cols) in enumerate(((pre, adv_taps), ((hid_hi[...], hid_lo[...]), proj_taps))):
        raw = stacked(rows, cols, (1, 1))
        total = jnp.zeros((16, N), F32)
        for x in range(2):
            pair = jnp.concatenate(split(raw[16 * x : 16 * x + 16]), axis=0)
            pair = dot(pair, gather[kind, x], (1, 0))
            total = total + pair[:16] + pair[16:]
        gradients.append(total)
    lane = lanes()
    beside = jnp.logical_and(lane >= 82, lane < 123)
    spare = gradients[1][8:]
    part[0:8] = jnp.where(beside, roll(spare, 82), gradients[0][:8])
    part[8:16] = jnp.where(beside, roll(spare, 41), gradients[0][8:])
    part[16:24] = gradients[1][:8]
    got5 = exchange(4, members, 3, part, recv5)

    scattered[...] = dot(
        jnp.concatenate([*taps_first, taps_first[0]], axis=0),
        jnp.concatenate([pre[0], pre[0], pre[1]], axis=0),
        (0, 0),
    )
    for y in range(18):
        moved = []
        for dz in range(3):
            total = None
            for dy in range(3):
                if 0 <= y - dy < 16:
                    at = (3 * dy + dz) * 16
                    term = scattered[at : at + 16, N * (y - dy) : N * (y - dy) + N]
                    total = term if total is None else total + term
            moved.append(total if dz == 1 else roll(total, dz - 1))
        gpart[16 * y : 16 * y + 16] = moved[0] + moved[1] + moved[2]
    for x in range(4):
        for c in range(3):
            at = 4 * x + c
            gext[c, x + 1, 7:8] = gpart[at : at + 1]
            middle = gpart[pl.ds(16 + at, 16, stride=16), :]
            gext[c, x + 1, 8:24] = middle + proj_own[c, x - 1] if x in (1, 2) else middle
            gext[c, x + 1, 24:25] = gpart[272 + at : 273 + at]

    for c in range(3):
        hext[c, 0] = STEP * (jnp.maximum(vext[0, 1], 0.0) * gext[c, 1])
        hext[c, 5] = -STEP * (jnp.minimum(vext[0, 4], 0.0) * gext[c, 4])
    for x in range(1, 5):
        v = [vext[c, x] for c in range(3)]
        g = [gext[c, x] for c in range(3)]
        positive = [jnp.maximum(a, 0.0) for a in v]
        negative = [jnp.minimum(a, 0.0) for a in v]
        totals = [jnp.zeros((32, N), F32)] * 3
        slopes = []
        for j in range(3):
            slope = jnp.zeros((32, N), F32)
            for c in range(3):
                here = (positive[j] - negative[j]) * g[c]
                if j == 0:
                    ahead = jnp.maximum(vext[0, x + 1], 0.0) * gext[c, x + 1]
                    behind = jnp.minimum(vext[0, x - 1], 0.0) * gext[c, x - 1]
                    before, after = vext[c, x - 1], vext[c, x + 1]
                elif j == 1:
                    ahead = shift_rows(positive[1] * g[c], -1)
                    behind = shift_rows(negative[1] * g[c], 1)
                    before, after = shift_rows(v[c], 1), shift_rows(v[c], -1)
                else:
                    ahead = roll(positive[2] * g[c], -1)
                    behind = roll(negative[2] * g[c], 1)
                    before, after = roll(v[c], 1), roll(v[c], -1)
                totals[c] = totals[c] + here - ahead + behind
                rising, falling = v[c] - before, after - v[c]
                level_slope = 0.5 * (rising + falling)
                slope = slope + g[c] * jnp.where(
                    v[j] > 0.0, rising, jnp.where(v[j] < 0.0, falling, level_slope)
                )
            slopes.append(slope)
        for c in range(3):
            hext[c, x] = g[c] - STEP * totals[c] - STEP * slopes[c]

    got5()

    def fold(ref):
        count = ref.shape[0] // 3
        return [
            jnp.sum(ref[pl.ds(row, count, stride=3), :], axis=0, keepdims=True) for row in range(3)
        ]

    for row, total in enumerate(fold(recv5)):
        mine[row : row + 1] = total
    got6 = exchange(5, heights, 3, mine, recv6)

    before_x, own_x, after_x = pl.ds(0, 2), pl.ds(2, 2), pl.ds(4, 2)
    before_y, own_y, after_y = pl.ds(6, 2), pl.ds(8, 16), pl.ds(24, 2)
    first_y, last_y = pl.ds(0, 2), pl.ds(6, 2)
    shared = copies(
        [
            (hext.at[:, after_x, own_y, :], face_x.at[0], (ahead_w, n)),
            (hext.at[:, before_x, own_y, :], face_x.at[1], (behind_w, n)),
            (hext.at[:, own_x, after_y, :], face_y.at[0, :, :, first_y, :], (w, above)),
            (hext.at[:, own_x, before_y, :], face_y.at[1, :, :, last_y, :], (w, below)),
            (hext.at[:, after_x, after_y, :], corner.at[0, :, :, first_y, :], (ahead_w, above)),
            (hext.at[:, after_x, before_y, :], corner.at[1, :, :, last_y, :], (ahead_w, below)),
            (hext.at[:, before_x, after_y, :], corner.at[2, :, :, first_y, :], (behind_w, above)),
            (hext.at[:, before_x, before_y, :], corner.at[3, :, :, last_y, :], (behind_w, below)),
        ],
        e1_send,
        e1_recv,
    )

    got6()
    for row, total in enumerate(fold(recv6)):
        whole[row : row + 1] = total * (N * N * N) ** -0.5
    got7 = exchange(6, level, 3, whole, sums_hbm)

    for copy in shared:
        copy.wait_recv()
    for c in range(3):
        for x in range(2):
            own = hext[c, x + 2, 8:24] + face_x[0, c, x] + face_x[1, c, x]
            out[c, x, 0:8] = own[0:8] + face_y[0, c, x] + corner[0, c, x] + corner[2, c, x]
            out[c, x, 8:16] = own[8:16] + face_y[1, c, x] + corner[1, c, x] + corner[3, c, x]
    store = pltpu.make_async_copy(out, out_hbm, load_sem.at[7 + TABLES])
    store.start()
    for wait in pending[:-1]:
        wait()
    store.wait()
    got7()
    pending[-1]()


def hand_out(grad, sums, out, out_first, out_bias, out_second):
    out[...] = grad[...]
    lane = lanes()
    total = sums[0:24] + sums[24:48] + sums[48:72] + sums[72:96]
    spare = jnp.where(lane < 41, roll(total[0:8], -82), roll(total[8:16], -41))
    both = (total[0:16], jnp.concatenate([total[16:24], spare], axis=0))
    for kind, ref in enumerate((out_first, out_second)):
        turned = both[kind].T
        for tap in range(27):
            ref[tap // 9, tap // 3 % 3, tap % 3] = turned[3 * tap : 3 * tap + 3]
        if kind == 0:
            out_bias[...] = turned[81:82]


def local(velocity, cotangents, lead_table, lead_index, first_kernel, first_bias, second_kernel):
    constants = tables()

    def v(*shape, kind=F32):
        return pltpu.VMEM(shape, kind)

    dma = pltpu.SemaphoreType.DMA
    in_vmem = pl.BlockSpec(memory_space=pltpu.VMEM)
    anywhere = pl.BlockSpec(memory_space=pl.ANY)
    shapes = tuple(
        jax.ShapeDtypeStruct(shape, F32)
        for shape in ((3, 2, 16, N), (3, 3, 3, 3, 16), (1, 16), (3, 3, 3, 3, 16))
    )
    results = pl.pallas_call(
        kernel,
        out_shape=(shapes[0], jax.ShapeDtypeStruct((96, N), F32)),
        in_specs=[anywhere] * (7 + TABLES),
        out_specs=(anywhere,) * 2,
        scratch_shapes=[
            v(4, 3, 2, 16, N), pltpu.SMEM((8,), F32), pltpu.SMEM((4,), jnp.int32),
            v(3, 3, 3, 3, 16), v(1, 16), v(3, 3, 3, 3, 16),
            *[v(*t.shape, kind=BF16) for t in constants],
            v(128, N), v(128, N), v(128, N), v(128, N), v(192, N), v(192, N), v(384, N), v(384, N),
            v(24, N), v(24, N), v(3, N), v(48, N), v(3, N), v(3, 2, 16, N),
            v(3, 6, 32, N), v(288, N), v(288, N), v(3, 2, 16, N),
            v(144, 2048, kind=BF16), v(144, 2048, kind=BF16),
            v(144, 2048, kind=BF16), v(144, 2048, kind=BF16),
            v(32, 2048), v(32, 2048, kind=BF16), v(32, 2048, kind=BF16),
            v(144, 2048), v(288, N), v(3, 6, 32, N),
            v(2, 3, 2, 16, N), v(2, 3, 2, 8, N), v(4, 3, 2, 8, N), v(3, 6, 32, N),
            v(N, N), dma((7,)), dma((7,)), dma((7,)), dma((8,)), dma((8,)), dma((8,)), dma((8,)),
            dma((8 + TABLES,)), pltpu.SemaphoreType.REGULAR,
        ],
        compiler_params=pltpu.CompilerParams(
            collective_id=0, has_side_effects=True, vmem_limit_bytes=60 * 1024 * 1024
        ),
        name="step_backward",
    )(
        cotangents, velocity, lead_table, lead_index,
        jnp.transpose(first_kernel, (1, 2, 3, 4, 0)), first_bias[None],
        jnp.transpose(second_kernel, (0, 2, 3, 4, 1)), *[jnp.asarray(t) for t in constants],
    )
    grad, first, bias, second = pl.pallas_call(
        hand_out,
        out_shape=shapes,
        in_specs=[in_vmem] * 2,
        out_specs=(in_vmem,) * 4,
        name="hand_out",
    )(*results)
    return (
        grad,
        jnp.transpose(first, (4, 0, 1, 2, 3)),
        bias[0],
        jnp.transpose(second, (0, 4, 1, 2, 3)),
    )


def solution(mesh):
    placed = (
        P(None, "wide", "narrow", None),
        P(None, None, "wide", "narrow", None),
        P(),
        P(),
        P(),
        P(),
        P(),
    )
    return jax.shard_map(
        local,
        mesh=mesh,
        in_specs=placed,
        out_specs=(P(None, "wide", "narrow", None), P(), P(), P()),
        check_vma=False,
    )
```
